256 devices in a mesh: comp: 8 (over y, core), lat: 32 (over x, z).
Axes of the slice: x: 4, y: 4, z: 8, core: 2. Of those that a mesh axis runs over, the one named last changes fastest.
Arguments:
- spectra_in: float32 [8, 36, 196608], P(None, None, ('comp', 'lat')), may hold values from 0 to 2
- group_speed: float32 [8, 256, 1024], P('comp', 'lat'), may hold values from 0.3 to 0.9
- turn_rate: float32 [8, 256, 1024], P('comp', 'lat'), may hold values from -0.9 to 0.9
- sea_mask: int32 [256, 1024], P('lat'), may hold values from 0 to 1, as said below
- sea_cell: int32 [196608], P('lat'), may hold values from 0 to 8191, as said below
- slab_counts: int32 [32], replicated, may hold values from 3072 to 6144, as said below
Outputs:
- spectra_out: float32 [8, 36, 196608], P(None, None, ('comp', 'lat'))
The draws below stay inside these ranges and needn't reach their ends.
Inputs may be any that keep to these rules, and one draw needn't show every extreme that they name: `sea_mask`: 1 at sea cells, 0 at land cells; slab l has slab_counts[l] sea cells. `sea_cell`: entries l * 6144 + p for p below slab_counts[l] are the indices (row in slab * 1024 + column) of slab l's sea cells in increasing order; the other entries of the slab name land cells. `slab_counts`: one slab holds exactly 6144 sea points and another exactly 3072.
All inputs are finite; a program needn't handle non-finite values.
Results may differ from the reference program's by a relative error of at most 0.0003.
Values sent between devices are 32-bit elements; how exact they have to be, the bound alone decides.
A program may use at most 128 MiB of HBM per device.

```python
import math
import jax
import jax.numpy as jnp
from jax import lax

NDIR = 36
NX = 1024
SUBSTEPS = 2
NFREQ = 8
NY = 256
CELLS = 8192
SEA_MAX = 6144
PT_DEV = 768
POINTS = 196608
N_LAT = 32
DEVICES = 256


def slab_ranks(rank_key):
    return jax.random.permutation(rank_key, CELLS)


def landscape(key):
    count_key, order_key, rank_key = jax.random.split(key, 3)
    counts = jax.random.randint(count_key, (N_LAT,), SEA_MAX // 2, SEA_MAX + 1).astype(jnp.int32)
    slab_order = jax.random.permutation(order_key, N_LAT)
    counts = counts.at[slab_order[0]].set(SEA_MAX).at[slab_order[1]].set(SEA_MAX // 2)
    cell_ranks = jax.vmap(slab_ranks)(jax.random.split(rank_key, N_LAT))
    is_sea = (cell_ranks < counts[:, None]).astype(jnp.int32)
    cells = jnp.argsort(1 - is_sea, axis=1, stable=True)[:, :SEA_MAX].astype(jnp.int32)
    return (counts, is_sea, cells)


def draw_sea_mask(key, part):
    counts, is_sea, cells = landscape(key)
    return is_sea.reshape(NY, NX).astype(jnp.int32)


def draw_sea_cell(key, part):
    counts, is_sea, cells = landscape(key)
    return cells.reshape(N_LAT * SEA_MAX).astype(jnp.int32)


def draw_slab_counts(key, part):
    counts, is_sea, cells = landscape(key)
    return counts.astype(jnp.int32)


def steps_of(key, shape, cuts, low, largest):
    def one(position, parts):
        steps = jax.random.uniform(jax.random.fold_in(jax.random.fold_in(key, 6), position), (parts,), jnp.float32, low / len(cuts), largest / len(cuts))
        return jnp.repeat(jnp.exp(steps), shape[position] // parts).reshape((-1,) + (1,) * (len(shape) - position - 1))

    gain = one(*cuts[0])
    for cut in cuts[1:]:
        gain = gain * one(*cut)
    return gain


def setup_inputs(seed: int = 0) -> dict:
    key_of = jax.random.split(jax.random.key(seed), 7)
    return {
        "spectra_in": jnp.clip(2.0 * jax.random.uniform(key_of[0], (NFREQ, NDIR, POINTS), jnp.float32) ** steps_of(key_of[0], (NFREQ, NDIR, POINTS), ((2, 256),), -0.2, 0.2), 0.0, 2.0),
        "group_speed": jnp.clip(0.3 + 0.59999996 * jax.random.uniform(key_of[1], (NFREQ, NY, NX), jnp.float32) ** steps_of(key_of[1], (NFREQ, NY, NX), ((0, 8), (1, 32)), -0.2, 0.2), 0.3, 0.9),
        "turn_rate": jnp.clip(jax.random.uniform(key_of[2], (NFREQ, NY, NX), jnp.float32, -0.9, 0.9) * steps_of(key_of[2], (NFREQ, NY, NX), ((0, 8), (1, 32)), -0.4, 0.0), -0.9, 0.9),
        "sea_mask": draw_sea_mask(jax.random.fold_in(key_of[6], 71), 0),
        "sea_cell": draw_sea_cell(jax.random.fold_in(key_of[6], 71), 0),
        "slab_counts": draw_slab_counts(jax.random.fold_in(key_of[6], 71), 0),
    }


def quickest(padded, courant, axis_dim):
    extent = padded.shape[axis_dim] - 4

    def segment(start_at, count):
        return lax.slice_in_dim(padded, start_at, start_at + count, axis=axis_dim)

    west_far = segment(0, extent + 1)
    west_near = segment(1, extent + 1)
    east_near = segment(2, extent + 1)
    east_far = segment(3, extent + 1)
    curvature = jnp.where(courant >= 0.0, east_near - 2.0 * west_near + west_far, east_far - 2.0 * east_near + west_near)
    face_value = 0.5 * (west_near + east_near) - 0.5 * courant * (east_near - west_near) - (1.0 - courant * courant) / 6.0 * curvature
    fluxes = courant * face_value
    return segment(2, extent) - (lax.slice_in_dim(fluxes, 1, extent + 1, axis=axis_dim) - lax.slice_in_dim(fluxes, 0, extent, axis=axis_dim))


def sweep_x(energy, speed, sea_weight, cosines):
    courant = speed[:, None] * cosines[None, :, None, None]
    c_padded = jnp.pad(courant, ((0, 0), (0, 0), (0, 0), (1, 1)))
    w_padded = jnp.pad(sea_weight, ((0, 0), (0, 0), (1, 1)))[:, None]
    face_c = 0.5 * (c_padded[..., :-1] + c_padded[..., 1:]) * w_padded[..., :-1] * w_padded[..., 1:]
    padded = jnp.pad(energy, ((0, 0), (0, 0), (0, 0), (2, 2)))
    return quickest(padded, face_c, 3)


def sweep_y(energy_ext, speed, sea_weight, sines):
    row_total = energy_ext.shape[2]
    courant = speed[:, None] * sines[None, :, None, None]
    weight = sea_weight[:, None]
    face_c = 0.5 * (courant[:, :, 1:row_total - 2] + courant[:, :, 2:row_total - 1]) * weight[:, :, 1:row_total - 2] * weight[:, :, 2:row_total - 1]
    return quickest(energy_ext, face_c, 2)


def sweep_theta(energy, turn, sea_weight, cosines):
    courant = (turn * sea_weight)[:, None] * cosines[None, :, None, None]
    c_padded = jnp.concatenate([courant[:, -1:], courant, courant[:, :1]], axis=1)
    face_c = 0.5 * (c_padded[:, :-1] + c_padded[:, 1:])
    padded = jnp.concatenate([energy[:, -2:], energy, energy[:, :2]], axis=1)
    return quickest(padded, face_c, 1)


def reference(spectra_in, group_speed, turn_rate, sea_mask, sea_cell, slab_counts):
    slab_ends = jnp.cumsum(slab_counts).astype(jnp.int32)
    slab_starts = (slab_ends - slab_counts).astype(jnp.int32)
    global_point = jnp.arange(POINTS, dtype=jnp.int32)
    slab_of = jnp.minimum(jnp.sum((global_point[:, None] >= slab_ends[None, :]).astype(jnp.int32), axis=1), N_LAT - 1).astype(jnp.int32)
    is_valid = global_point < slab_ends[N_LAT - 1]
    slab_pos = jnp.clip(global_point - slab_starts[slab_of], 0, SEA_MAX - 1).astype(jnp.int32)
    grid_cell = (slab_of * CELLS + sea_cell[slab_of * SEA_MAX + slab_pos]).astype(jnp.int32)
    target = jnp.where(is_valid, grid_cell, NY * NX).astype(jnp.int32)
    slot_of = ((global_point % DEVICES) * PT_DEV + global_point // DEVICES).astype(jnp.int32)
    angles = jnp.arange(NDIR, dtype=jnp.float32) * (2.0 * math.pi / NDIR)
    cosines = jnp.cos(angles)
    sines = jnp.sin(angles)
    sea_weight = sea_mask.astype(jnp.float32)[None]
    row_pad = ((0, 0), (2, 2), (0, 0))

    def one_freq(inputs):
        spectrum, speed, turn = inputs
        flat_grid = jnp.zeros((NDIR, NY * NX), jnp.float32).at[:, target].set(spectrum[:, slot_of], mode="drop")
        energy = flat_grid.reshape(1, NDIR, NY, NX)
        speed_one = speed[None]
        turn_one = turn[None]
        speed_pad = jnp.pad(speed_one, row_pad)
        weight_pad = jnp.pad(sea_weight, row_pad)
        for substep in range(SUBSTEPS):
            energy = sweep_x(energy, speed_one, sea_weight, cosines)
            energy = sweep_y(jnp.pad(energy, ((0, 0), (0, 0), (2, 2), (0, 0))), speed_pad, weight_pad, sines)
            energy = sweep_theta(energy, turn_one, sea_weight, cosines)
        flat_grid = energy.reshape(NDIR, NY * NX)
        values = jnp.where(is_valid[None], flat_grid[:, grid_cell], jnp.zeros((), jnp.float32))
        return jnp.zeros((NDIR, POINTS), jnp.float32).at[:, slot_of].set(values)

    return lax.map(one_freq, (spectra_in, group_speed, turn_rate))
```

```python
import math

import jax
import jax.numpy as jnp
import numpy as np
from jax import lax
from jax.experimental import pallas as pl
from jax.experimental.pallas import tpu as pltpu
from jax.sharding import PartitionSpec as P

NC = 8
NL = 32
ND = 36
SLOTS = 768
BUCKET = 24
ROWS = 8
FOLD = 5
TILES = 7
LAST = ND - 1
CHUNKS = ((32, 4), (0, 8), (8, 8), (16, 8), (24, 8))
GROUPS = ((0, 2), (2, 2), (4, 3))
PIECES = ((0, 32), (32, 4))
SIN_POS = 19

ANGLES = np.arange(ND, dtype=np.float32) * np.float32(2.0 * math.pi / ND)
COS = np.cos(ANGLES).astype(np.float32)
SIN = np.sin(ANGLES).astype(np.float32)
TURN = (0.5 * (COS + np.roll(COS, -1))).astype(np.float32)
assert (SIN[:SIN_POS] >= 0).all() and (SIN[SIN_POS:] < 0).all()

SLOT_TILES = ((0,), (0, 1), (0, 1, 2), (1, 2, 3), (1, 2, 3, 4), (2, 3, 4, 5), (2, 3, 4, 5))
POINT_TILES = tuple(
    tuple(range(max(0, 4 * v - 20) // 8, min(2, (4 * v + 3) // 8) + 1)) for v in range(ROWS)
)
ROW_TILES = tuple(tuple(range(2 * u, min(7, 2 * u + 6) + 1)) for u in range(3))


def lanes(values, index):
    return jnp.take_along_axis(values, index, axis=1)


def sublanes(values, index):
    return jnp.take_along_axis(values, index, axis=0)


def iotas():
    return (
        lax.broadcasted_iota(jnp.int32, (8, 128), 0),
        lax.broadcasted_iota(jnp.int32, (8, 128), 1),
    )


def swap_blocks(parts, block_masks, turns):
    rolled = []
    for k in range(FOLD):
        diagonal = parts[(FOLD - 1 + k) % FOLD]
        for b in range(FOLD - 1):
            diagonal = jnp.where(block_masks[b], parts[(b + k) % FOLD], diagonal)
        rolled.append(diagonal if k == 0 else lanes(diagonal, turns[k]))
    outs = []
    for a in range(FOLD):
        value = rolled[(FOLD - 1 - a) % FOLD]
        for b in range(FOLD - 1):
            value = jnp.where(block_masks[b], rolled[(b - a) % FOLD], value)
        outs.append(value)
    return outs


def flux(q, d, curvature, c):
    sixth = 1.0 / 6.0
    return c * (q + (1.0 - c) * (0.5 * d - (c * sixth + sixth) * curvature))


def sweep_x(q, c, sign, sub, lane):
    east = lanes(q, (lane + 1) & 127)
    east = jnp.where(lane == 127, sublanes(east, (sub + 1) & 7), east)
    east = jnp.where((lane == 127) & (sub == 7), 0.0, east)
    d = east - q
    side = lanes(d, (lane - sign) & 127)
    edge = lane == jnp.where(sign > 0, 0, 127)
    side = jnp.where(edge, sublanes(side, (sub - sign) & 7), side)
    side = jnp.where(edge & (sub == jnp.where(sign > 0, 0, 7)), q, side)
    curvature = (d - side) * jnp.where(sign > 0, 1.0, -1.0)
    f = flux(q, d, curvature, c)
    west = lanes(f, (lane - 1) & 127)
    west = jnp.where(lane == 0, sublanes(west, (sub - 1) & 7), west)
    return q - (f - west)


def kernel(
    spectra, speed, turn, mask, cells, counts, trig, out,
    a_buf, m_buf, r_buf, p_buf, n_buf, o_buf, x_ext, y_buf,
    spd, trn, msk, stat_halo, sx, sy,
    pack_at, put_at, put_tile, row_at, row_tile, lane_at, take_at, back_row, back_tile, w_last,
    first_send, first_recv, first_own, second_send, second_recv, second_own,
    stat_send, stat_recv, halo_send, halo_recv,
    third_send, third_recv, third_own, fourth_send, fourth_recv, fourth_own,
):
    me_c = lax.axis_index("comp")
    me_l = lax.axis_index("lat")
    sub, lane = iotas()

    def slot_of(c):
        return (c % 4) * 2 + c // 4

    def first_ends(g, peer):
        part = pl.ds(*CHUNKS[g])
        return spectra.at[part, peer, :], a_buf.at[part, slot_of(me_c), :]

    def first_local(g):
        source_ref, target_ref = first_ends(g, me_c)
        return pltpu.make_async_copy(source_ref, target_ref, first_own.at[g])

    for g in range(len(CHUNKS)):
        first_local(g).start()

    barrier = pltpu.get_barrier_semaphore()

    def greet_comp(r, carry):
        pl.semaphore_signal(
            barrier, inc=1, device_id={"comp": (me_c + r) % NC, "lat": me_l}, device_id_type=pl.DeviceIdType.MESH
        )
        return carry

    def greet_lat(r, carry):
        pl.semaphore_signal(
            barrier, inc=1, device_id={"comp": me_c, "lat": (me_l + r) % NL}, device_id_type=pl.DeviceIdType.MESH
        )
        return carry

    lax.fori_loop(1, NC, greet_comp, 0)
    lax.fori_loop(1, NL, greet_lat, 0)

    starts = [jnp.int32(0)]
    for slab in range(NL):
        starts.append(starts[-1] + counts[slab])
    own_start = jnp.int32(0)
    for slab in range(NL):
        own_start = own_start + jnp.where(slab < me_l, counts[slab], 0)

    source = ((sub & 1) * 4 + (sub >> 1)) * NL + me_l
    block = (lane * 171) >> 12
    in_block = lane - block * BUCKET
    block_masks = [block == b for b in range(FOLD)]
    turns = [None] + [
        jnp.where(lane >= BUCKET * k, lane - BUCKET * k, lane - BUCKET * k + BUCKET * FOLD) & 127
        for k in range(1, FOLD)
    ]
    for v in range(TILES):
        base = jnp.full((8, 128), starts[min(FOLD * v, NL - 1)], jnp.int32)
        for b in range(1, FOLD):
            if FOLD * v + b < NL:
                base = jnp.where(block == b, starts[FOLD * v + b], base)
        pack_at[v] = ((base - source + 255) >> 8) + in_block

    for t in range(8):
        columns = pl.ds(128 * t, 128)
        spd[pl.ds(t, 8, stride=8), :] = speed[0, :, columns]
        trn[pl.ds(t, 8, stride=8), :] = turn[0, :, columns]
        msk[pl.ds(t, 8, stride=8), :] = mask[:, columns].astype(jnp.float32)

    pl.semaphore_wait(barrier, NC - 1 + NL - 1)

    def first_copy(g, r):
        peer = (me_c + r) % NC
        source_ref, target_ref = first_ends(g, peer)
        return pltpu.make_async_remote_copy(
            src_ref=source_ref,
            dst_ref=target_ref,
            send_sem=first_send.at[g],
            recv_sem=first_recv.at[g],
            device_id={"comp": peer, "lat": me_l},
            device_id_type=pl.DeviceIdType.MESH,
        )

    for g in range(len(CHUNKS)):
        for r in range(1, NC):
            first_copy(g, r).start()

    north = {"comp": me_c, "lat": (me_l + 1) % NL}
    south = {"comp": me_c, "lat": (me_l + NL - 1) % NL}

    def stat_copy(k):
        ref = (spd, msk)[k % 2]
        row = 56 if k < 2 else 0
        return pltpu.make_async_remote_copy(
            src_ref=ref.at[pl.ds(row, 8), :],
            dst_ref=stat_halo.at[k],
            send_sem=stat_send.at[k],
            recv_sem=stat_recv.at[k],
            device_id=north if k < 2 else south,
            device_id_type=pl.DeviceIdType.MESH,
        )

    for k in range(4):
        stat_copy(k).start()

    def first_wait(g, sem):
        low, size = CHUNKS[g]
        ref = a_buf.at[pl.ds(low, size), pl.ds(0, NC - 1), :]
        return pltpu.make_async_copy(ref, ref, sem.at[g])

    for u in range(6):
        point = source + (lane + 128 * u) * 256
        slab = jnp.zeros((8, 128), jnp.int32)
        begin = jnp.zeros((8, 128), jnp.int32)
        for s in range(1, NL + 1):
            past = point >= starts[s]
            slab = jnp.where(past, s, slab)
            begin = jnp.where(past, starts[s], begin)
        nth = lane + 128 * u - ((begin - source + 255) >> 8)
        tile = (slab * 205) >> 10
        put_at[u] = ((slab - tile * FOLD) * BUCKET + nth) & 127
        put_tile[u] = jnp.where(slab < NL, tile, -1)

    ones = jnp.ones((128, 128), jnp.bfloat16)
    deep = lax.broadcasted_iota(jnp.int32, (128, 128), 0)
    wide = lax.broadcasted_iota(jnp.int32, (128, 128), 1)
    before = jnp.where(deep < wide, 1.0, 0.0).astype(jnp.bfloat16)
    above = jnp.where(wide < deep, 1.0, 0.0).astype(jnp.bfloat16)[:64, :64]
    sea = msk[...].astype(jnp.bfloat16)
    inside = jnp.dot(sea, before, preferred_element_type=jnp.float32)
    totals = jnp.dot(sea, ones, preferred_element_type=jnp.float32)
    offsets = jnp.dot(above, totals.astype(jnp.bfloat16), preferred_element_type=jnp.float32)
    inside = inside.astype(jnp.int32)
    offsets = offsets.astype(jnp.int32)
    low_source = (lane & 3) * NL + (lane >> 2)
    for v in range(ROWS):
        offset = offsets[8 * v : 8 * v + 8]
        point = offset + inside[8 * v : 8 * v + 8] + own_start
        lane_at[v] = ((point & 31) << 2) | ((point >> 5) & 3)
        point = offset + ((low_source - own_start - offset) & 127)
        row_at[v] = (point >> 8) & 7
        row_tile[v] = ((point >> 11) << 1) + (((point + own_start) >> 7) & 1)
    cell_at = []
    for u in range(3):
        even = cells[pl.ds(16 * u, 8, stride=2), :]
        odd = cells[pl.ds(16 * u + 1, 8, stride=2), :]
        for h in range(2):
            rho = (low_source + 128 * h - own_start) & 255
            cell = jnp.where(rho < 128, lanes(even, rho & 127), lanes(odd, rho & 127))
            cell_at.append(cell)
            back_row[u, h] = (cell >> 7) & 7
            back_tile[u, h] = cell >> 10
    for v in range(ROWS):
        index = row_at[v]
        which = row_tile[v]
        value = jnp.zeros((8, 128), jnp.int32)
        for u in POINT_TILES[v]:
            for h in range(2):
                value = jnp.where(which == 2 * u + h, sublanes(cell_at[2 * u + h], index), value)
        take_at[v] = value & 127

    for v in range(ROWS):
        rows = pl.ds(8 * v, 8)
        s = spd[rows, :]
        m = msk[rows, :]

        def eastward(x):
            east = lanes(x, (lane + 1) & 127)
            return jnp.where(lane == 127, sublanes(east, (sub + 1) & 7), east)

        face = 0.5 * (s + eastward(s)) * m * eastward(m)
        sx[v] = jnp.where((lane == 127) & (sub == 7), 0.0, face)
        trn[rows, :] = trn[rows, :] * m
        if v < ROWS - 1:
            after = pl.ds(8 * v + 8, 8)
            sy[v + 1] = 0.5 * (s + spd[after, :]) * m * msk[after, :]
    for k in range(4):
        stat_copy(k).wait()
    south_mask = jnp.where(me_l > 0, stat_halo[1], 0.0)
    north_mask = jnp.where(me_l < NL - 1, stat_halo[3], 0.0)
    sy[0] = 0.5 * (stat_halo[0] + spd[0:8, :]) * south_mask * msk[0:8, :]
    sy[8] = 0.5 * (stat_halo[2] + spd[56:64, :]) * north_mask * msk[56:64, :]

    def a_rows(direction):
        return [a_buf[direction, :, pl.ds(128 * u, 128)] for u in range(6)]

    def windows(direction, v, rows):
        at = pack_at[v]
        low = at & 127
        value = None
        for u in SLOT_TILES[v]:
            got = lanes(rows[u], low)
            value = got if value is None else jnp.where((at >> 7) == u, got, value)
        return value

    def second_copy(k, r):
        low, size = GROUPS[k]
        peer = (me_l + r) % NL
        return pltpu.make_async_remote_copy(
            src_ref=m_buf.at[peer, pl.ds(low, size)],
            dst_ref=r_buf.at[pl.ds(low, size), me_l],
            send_sem=second_send.at[k],
            recv_sem=second_recv.at[k],
            device_id={"comp": me_c, "lat": peer},
            device_id_type=pl.DeviceIdType.MESH,
        )

    def second_local(k):
        low, size = GROUPS[k]
        return pltpu.make_async_copy(
            m_buf.at[me_l, pl.ds(low, size)], r_buf.at[pl.ds(low, size), me_l], second_own.at[k]
        )

    def many(ref, k, sem):
        low, size = GROUPS[k]
        part = ref.at[pl.ds(low, size), pl.ds(0, NL - 1)]
        return pltpu.make_async_copy(part, part, sem.at[k])

    def pack_tile(tile, carry):
        rows = [a_rows(FOLD * tile + s) for s in range(FOLD)]
        octet = jnp.minimum(tile, 2) * 8
        for v in range(TILES):
            parts = [windows(FOLD * tile + s, v, rows[s]) for s in range(FOLD)]
            spare = w_last[v]
            for b, value in enumerate(swap_blocks(parts, block_masks, turns)):
                if FOLD * v + b < NL:
                    extra = lanes(spare, BUCKET * b + octet + (lane & 7))
                    m_buf[FOLD * v + b, tile] = jnp.where(lane >= 120, extra, value)
        return carry

    def arrived(g):
        first_wait(g, first_recv).wait()
        first_local(g).wait()

    arrived(0)
    rows = a_rows(LAST)
    for v in range(TILES):
        w_last[v] = windows(LAST, v, rows)
    waited = 1
    for k, (low, size) in enumerate(GROUPS):
        need = min(FOLD * (low + size) - 1, 31) // 8 + 1
        while waited <= need:
            arrived(waited)
            waited += 1
        lax.fori_loop(low, low + size, pack_tile, 0)

        def send(r, carry, k=k):
            second_copy(k, r).start()
            return carry

        lax.fori_loop(1, NL, send, 0)
        second_local(k).start()

    r_rows = r_buf.reshape(TILES, NL * 8, 128)

    def turn_in(tile, carry):
        for h in range(2):
            p_buf[tile, h] = r_rows[tile, pl.ds(h, 128, stride=2), :].T
        return carry

    for k, (low, size) in enumerate(GROUPS):
        many(r_buf, k, second_recv).wait()
        second_local(k).wait()
        lax.fori_loop(low, low + size, turn_in, 0)

    def point_rows(tile, s, u, h):
        if s is None:
            return p_buf[u, h, 120:128, :]
        return p_buf[tile, h, BUCKET * s + 8 * u : BUCKET * s + 8 * u + 8, :]

    def place(direction, tile, s):
        held = {(u, h): point_rows(tile, s, u, h) for u in range(3) for h in range(2)}
        cosine = trig[0, direction]
        sign = jnp.where(cosine >= 0.0, 1, -1)
        for v in range(ROWS):
            index = row_at[v]
            which = row_tile[v]
            value = None
            for u in POINT_TILES[v]:
                for h in range(2):
                    got = sublanes(held[u, h], index)
                    value = got if value is None else jnp.where(which == 2 * u + h, got, value)
            q = jnp.where(msk[pl.ds(8 * v, 8), :] > 0.0, lanes(value, lane_at[v]), 0.0)
            x_ext[0, direction, v + 2] = sweep_x(q, cosine * sx[v], sign, sub, lane)

    def place_tile(tile, carry):
        for s in range(FOLD):
            place(FOLD * tile + s, tile, s)
        return carry

    lax.fori_loop(0, TILES, place_tile, 0)
    place(LAST, None, None)

    def halo_copy(step, k):
        positive = pl.ds(0, SIN_POS)
        negative = pl.ds(SIN_POS, ND - SIN_POS)
        which, source_rows, target_rows, peer = (
            (positive, pl.ds(8, 2), pl.ds(0, 2), north),
            (negative, pl.ds(9, 1), pl.ds(1, 1), north),
            (positive, pl.ds(2, 1), pl.ds(10, 1), south),
            (negative, pl.ds(2, 2), pl.ds(10, 2), south),
        )[k]
        return pltpu.make_async_remote_copy(
            src_ref=x_ext.at[step, which, source_rows],
            dst_ref=x_ext.at[step, which, target_rows],
            send_sem=halo_send.at[step, k],
            recv_sem=halo_recv.at[step, k],
            device_id=peer,
            device_id_type=pl.DeviceIdType.MESH,
        )

    def sweep_y(step, positive, row_list):
        def body(direction, carry):
            sine = trig[1, direction]

            def row(r):
                value = x_ext[step, direction, r + 2]
                if r < 0:
                    value = jnp.where(me_l > 0, value, 0.0)
                if r >= ROWS:
                    value = jnp.where(me_l < NL - 1, value, 0.0)
                return value

            diffs = {}
            fluxes = {}

            def diff(f):
                if f not in diffs:
                    diffs[f] = row(f) - row(f - 1)
                return diffs[f]

            def face(f):
                if f not in fluxes:
                    if positive:
                        curvature = diff(f) - diff(f - 1)
                    else:
                        curvature = diff(f + 1) - diff(f)
                    fluxes[f] = flux(row(f - 1), diff(f), curvature, sine * sy[f])
                return fluxes[f]

            for r in row_list:
                y_buf[direction, r] = row(r) - (face(r + 1) - face(r))
            return carry

        if positive:
            lax.fori_loop(0, SIN_POS, body, 0)
        else:
            lax.fori_loop(SIN_POS, ND, body, 0)

    def sweep_theta(step, r):
        t = trn[pl.ds(pl.multiple_of(8 * r, 8), 8), :]
        forward = t >= 0.0
        q = [y_buf[j, r] for j in range(ND)]
        d = [q[(j + 1) % ND] - q[j] for j in range(ND)]

        def face(j):
            ahead = d[(j + 1) % ND] - d[j]
            behind = d[j] - d[j - 1]
            if TURN[j] >= 0:
                curvature = jnp.where(forward, behind, ahead)
            else:
                curvature = jnp.where(forward, ahead, behind)
            return flux(q[j], d[j], curvature, float(TURN[j]) * t)

        last = face(ND - 1)
        prior = last
        for j in range(ND):
            f = last if j == ND - 1 else face(j)
            value = q[j] - (f - prior)
            prior = f
            if step == 0:
                sign = 1 if COS[j] >= 0 else -1
                x_ext[1, j, r + 2] = sweep_x(value, float(COS[j]) * sx[r], sign, sub, lane)
            else:
                y_buf[j, r] = value

    inner = tuple(range(2, 6))
    outer = (0, 1, 6, 7)
    for step in range(2):
        for k in range(4):
            halo_copy(step, k).start()
        sweep_y(step, True, inner)
        sweep_y(step, False, inner)

        def inner_rows(r, carry, step=step):
            sweep_theta(step, r)
            return carry

        def outer_rows(k, carry, step=step):
            sweep_theta(step, k + 4 * (k // 2))
            return carry

        lax.fori_loop(2, 6, inner_rows, 0)
        for k in range(4):
            halo_copy(step, k).wait()
        sweep_y(step, True, outer)
        sweep_y(step, False, outer)
        lax.fori_loop(0, 4, outer_rows, 0)

    def collect(direction, tile, s):
        taken = [lanes(y_buf[direction, v], take_at[v]) for v in range(ROWS)]
        for u in range(3):
            for h in range(2):
                index = back_row[u, h]
                which = back_tile[u, h]
                value = None
                for v in ROW_TILES[u]:
                    got = sublanes(taken[v], index)
                    value = got if value is None else jnp.where(which == v, got, value)
                if s is None:
                    p_buf[u, h, 120:128, :] = value
                else:
                    p_buf[tile, h, BUCKET * s + 8 * u : BUCKET * s + 8 * u + 8, :] = value

    def third_copy(k, r):
        low, size = GROUPS[k]
        peer = (me_l + r) % NL
        return pltpu.make_async_remote_copy(
            src_ref=m_buf.at[peer, pl.ds(low, size)],
            dst_ref=n_buf.at[pl.ds(low, size), me_l],
            send_sem=third_send.at[k],
            recv_sem=third_recv.at[k],
            device_id={"comp": me_c, "lat": peer},
            device_id_type=pl.DeviceIdType.MESH,
        )

    def third_local(k):
        low, size = GROUPS[k]
        return pltpu.make_async_copy(
            m_buf.at[me_l, pl.ds(low, size)], n_buf.at[pl.ds(low, size), me_l], third_own.at[k]
        )

    for k in range(len(GROUPS)):
        many(r_buf, k, second_send).wait()

    m_rows = m_buf.reshape(NL * TILES * 8, 128)

    def turn_out(tile, carry):
        for h in range(2):
            r_rows[tile, pl.ds(h, 128, stride=2), :] = p_buf[tile, h].T
        for l in range(NL):
            m_buf[l, tile] = r_buf[tile, l]
        return carry

    def collect_tile(tile, carry):
        for s in range(FOLD):
            collect(FOLD * tile + s, tile, s)
        turn_out(tile, 0)
        return carry

    collect(LAST, None, None)
    for k, (low, size) in enumerate(GROUPS):
        lax.fori_loop(low, low + size, collect_tile, 0)

        def send(r, carry, k=k):
            third_copy(k, r).start()
            return carry

        lax.fori_loop(1, NL, send, 0)
        third_local(k).start()

    def put(direction, parts):
        for u in range(6):
            at = put_at[u]
            which = put_tile[u]
            value = jnp.zeros((8, 128), jnp.float32)
            for v in range(TILES):
                if u in SLOT_TILES[v]:
                    value = jnp.where(which == v, lanes(parts[v], at), value)
            o_buf[direction, :, pl.ds(128 * u, 128)] = value

    def put_tile_of(tile, carry):
        swapped = []
        for v in range(TILES):
            parts = [n_buf[tile, min(FOLD * v + b, NL - 1)] for b in range(FOLD)]
            swapped.append(swap_blocks(parts, block_masks, turns))
        for s in range(FOLD):
            put(FOLD * tile + s, [swapped[v][s] for v in range(TILES)])
        return carry

    def put_last():
        parts = []
        spare = 120 + (lane & 7)
        for v in range(TILES):
            value = jnp.zeros((8, 128), jnp.float32)
            for b in range(FOLD):
                if FOLD * v + b < NL:
                    for e in range(3):
                        got = lanes(n_buf[e, FOLD * v + b], spare)
                        value = jnp.where((lane >> 3) == 3 * b + e, got, value)
            parts.append(value)
        put(LAST, parts)

    def fourth_ends(k, peer):
        part = pl.ds(*PIECES[k])
        return o_buf.at[part, slot_of(peer), :], out.at[part, me_c, :]

    def fourth_copy(k, r):
        peer = (me_c + r) % NC
        source_ref, target_ref = fourth_ends(k, peer)
        return pltpu.make_async_remote_copy(
            src_ref=source_ref,
            dst_ref=target_ref,
            send_sem=fourth_send.at[k],
            recv_sem=fourth_recv.at[k],
            device_id={"comp": peer, "lat": me_l},
            device_id_type=pl.DeviceIdType.MESH,
        )

    def fourth_local(k):
        source_ref, target_ref = fourth_ends(k, me_c)
        return pltpu.make_async_copy(source_ref, target_ref, fourth_own.at[k])

    for k, (low, size) in enumerate(GROUPS):
        many(n_buf, k, third_recv).wait()
        third_local(k).wait()
        lax.fori_loop(low, low + size, put_tile_of, 0)
    put_last()
    for k in range(len(PIECES)):
        for r in range(1, NC):
            fourth_copy(k, r).start()
        fourth_local(k).start()

    for g in range(len(CHUNKS)):
        first_wait(g, first_send).wait()
    for k in range(len(GROUPS)):
        many(n_buf, k, third_send).wait()
    for k, (low, size) in enumerate(PIECES):
        fourth_local(k).wait()
        part = out.at[pl.ds(low, size), pl.ds(0, NC - 1), :]
        pltpu.make_async_copy(part, part, fourth_recv.at[k]).wait()
        pltpu.make_async_copy(part, part, fourth_send.at[k]).wait()


def per_device(spectra_in, group_speed, turn_rate, sea_mask, sea_cell, slab_counts):
    f32 = jnp.float32
    vreg = (8, 128)
    dma = pltpu.SemaphoreType.DMA
    vmem = pl.BlockSpec(memory_space=pltpu.VMEM)
    smem = pl.BlockSpec(memory_space=pltpu.SMEM)
    anywhere = pl.BlockSpec(memory_space=pl.ANY)
    chunks, groups, pieces = len(CHUNKS), len(GROUPS), len(PIECES)
    return pl.pallas_call(
        kernel,
        out_shape=jax.ShapeDtypeStruct((ND, NC, SLOTS), f32),
        in_specs=[anywhere, vmem, vmem, vmem, vmem, smem, smem],
        out_specs=anywhere,
        scratch_shapes=[
            pltpu.VMEM((ND, NC, SLOTS), f32),
            pltpu.VMEM((NL, TILES) + vreg, f32),
            pltpu.VMEM((TILES, NL) + vreg, f32),
            pltpu.VMEM((TILES, 2, 128, 128), f32),
            pltpu.VMEM((TILES, NL) + vreg, f32),
            pltpu.VMEM((ND, NC, SLOTS), f32),
            pltpu.VMEM((2, ND, ROWS + 4) + vreg, f32),
            pltpu.VMEM((ND, ROWS) + vreg, f32),
            pltpu.VMEM((64, 128), f32),
            pltpu.VMEM((64, 128), f32),
            pltpu.VMEM((64, 128), f32),
            pltpu.VMEM((4,) + vreg, f32),
            pltpu.VMEM((ROWS,) + vreg, f32),
            pltpu.VMEM((ROWS + 1,) + vreg, f32),
            pltpu.VMEM((TILES,) + vreg, jnp.int32),
            pltpu.VMEM((6,) + vreg, jnp.int32),
            pltpu.VMEM((6,) + vreg, jnp.int32),
            pltpu.VMEM((ROWS,) + vreg, jnp.int32),
            pltpu.VMEM((ROWS,) + vreg, jnp.int32),
            pltpu.VMEM((ROWS,) + vreg, jnp.int32),
            pltpu.VMEM((ROWS,) + vreg, jnp.int32),
            pltpu.VMEM((3, 2) + vreg, jnp.int32),
            pltpu.VMEM((3, 2) + vreg, jnp.int32),
            pltpu.VMEM((TILES,) + vreg, f32),
            dma((chunks,)), dma((chunks,)), dma((chunks,)),
            dma((groups,)), dma((groups,)), dma((groups,)),
            dma((4,)), dma((4,)), dma((2, 4)), dma((2, 4)),
            dma((groups,)), dma((groups,)), dma((groups,)),
            dma((pieces,)), dma((pieces,)), dma((pieces,)),
        ],
        compiler_params=pltpu.CompilerParams(
            collective_id=0, has_side_effects=True, vmem_limit_bytes=40 * 1024 * 1024
        ),
        name="wave_step",
    )(
        spectra_in.transpose(1, 0, 2),
        group_speed,
        turn_rate,
        sea_mask,
        sea_cell.reshape(48, 128),
        slab_counts,
        jnp.asarray(np.stack([COS, SIN])),
    ).transpose(1, 0, 2)


def solution(mesh):
    in_specs = (
        P(None, None, ("comp", "lat")),
        P("comp", "lat", None),
        P("comp", "lat", None),
        P("lat", None),
        P("lat"),
        P(),
    )
    out_specs = P(None, None, ("comp", "lat"))
    return jax.shard_map(
        per_device, mesh=mesh, in_specs=in_specs, out_specs=out_specs, check_vma=False
    )
```

```python
import math

import jax
import jax.numpy as jnp
import numpy as np
from jax import lax
from jax.experimental import pallas as pl
from jax.experimental.pallas import tpu as pltpu
from jax.sharding import PartitionSpec as P

NC = 8
NL = 32
ND = 36
SLOTS = 768
BUCKET = 24
ROWS = 8
FOLD = 5
TILES = 7
LAST = ND - 1
SIN_POS = 19

ANGLES = np.arange(ND, dtype=np.float32) * np.float32(2.0 * math.pi / ND)
COS = np.cos(ANGLES).astype(np.float32)
SIN = np.sin(ANGLES).astype(np.float32)
TURN = (0.5 * (COS + np.roll(COS, -1))).astype(np.float32)
assert (SIN[:SIN_POS] >= 0).all() and (SIN[SIN_POS:] < 0).all()

SLOT_TILES = ((0,), (0, 1), (0, 1, 2), (1, 2, 3), (1, 2, 3, 4), (2, 3, 4, 5), (2, 3, 4, 5))
POINT_TILES = tuple(
    tuple(range(max(0, 4 * v - 20) // 8, min(2, (4 * v + 3) // 8) + 1)) for v in range(ROWS)
)
ROW_TILES = tuple(tuple(range(2 * u, min(7, 2 * u + 6) + 1)) for u in range(3))


def lanes(values, index):
    return jnp.take_along_axis(values, index, axis=1)


def sublanes(values, index):
    return jnp.take_along_axis(values, index, axis=0)


def iotas():
    return (
        lax.broadcasted_iota(jnp.int32, (8, 128), 0),
        lax.broadcasted_iota(jnp.int32, (8, 128), 1),
    )


def swap_blocks(parts, block_masks, turns):
    rolled = []
    for k in range(FOLD):
        diagonal = parts[(FOLD - 1 + k) % FOLD]
        for b in range(FOLD - 1):
            diagonal = jnp.where(block_masks[b], parts[(b + k) % FOLD], diagonal)
        rolled.append(diagonal if k == 0 else lanes(diagonal, turns[k]))
    outs = []
    for a in range(FOLD):
        value = rolled[(FOLD - 1 - a) % FOLD]
        for b in range(FOLD - 1):
            value = jnp.where(block_masks[b], rolled[(b - a) % FOLD], value)
        outs.append(value)
    return outs


def flux(q, d, curvature, c):
    sixth = 1.0 / 6.0
    return c * (q + (1.0 - c) * (0.5 * d - (c * sixth + sixth) * curvature))


def sweep_x(q, c, sign, sub, lane):
    east = lanes(q, (lane + 1) & 127)
    east = jnp.where(lane == 127, sublanes(east, (sub + 1) & 7), east)
    east = jnp.where((lane == 127) & (sub == 7), 0.0, east)
    d = east - q
    side = lanes(d, (lane - sign) & 127)
    edge = lane == jnp.where(sign > 0, 0, 127)
    side = jnp.where(edge, sublanes(side, (sub - sign) & 7), side)
    side = jnp.where(edge & (sub == jnp.where(sign > 0, 0, 7)), q, side)
    curvature = (d - side) * jnp.where(sign > 0, 1.0, -1.0)
    f = flux(q, d, curvature, c)
    west = lanes(f, (lane - 1) & 127)
    west = jnp.where(lane == 0, sublanes(west, (sub - 1) & 7), west)
    return q - (f - west)


def kernel(
    spectra, speed_in, turn_in, mask_in, cells_in, counts_in, out,
    speed, turn, mask, cells, counts, trig, load_sem,
    a_buf, m_buf, r_buf, p_buf, n_buf, o_buf, x_ext, y_buf,
    spd, trn, msk, stat_halo, sx, sy,
    pack_at, put_at, put_tile, row_at, row_tile, lane_at, take_at, back_row, back_tile, w_last,
    first_send, first_recv, first_own, second_send, second_recv, second_own,
    stat_send, stat_recv, halo_send, halo_recv,
    third_send, third_recv, third_own, fourth_send, fourth_recv, fourth_own,
):
    me_c = lax.axis_index("comp")
    me_l = lax.axis_index("lat")
    sub, lane = iotas()

    def slot_of(c):
        return (c % 4) * 2 + c // 4

    loads = [
        pltpu.make_async_copy(source_ref, target_ref, load_sem.at[k])
        for k, (source_ref, target_ref) in enumerate(
            ((counts_in, counts), (speed_in, speed), (turn_in, turn), (mask_in, mask), (cells_in, cells))
        )
    ]
    for load in loads:
        load.start()

    def chunk(g):
        return pl.ds(FOLD * g, 1 if isinstance(g, int) and g == TILES else FOLD)

    def first_ends(g, peer):
        return spectra.at[chunk(g), peer, :], a_buf.at[chunk(g), slot_of(me_c), :]

    def first_local(g):
        source_ref, target_ref = first_ends(g, me_c)
        return pltpu.make_async_copy(source_ref, target_ref, first_own.at[g])

    for g in range(TILES + 1):
        first_local(g).start()

    barrier = pltpu.get_barrier_semaphore()

    def greet_comp(r, carry):
        pl.semaphore_signal(
            barrier, inc=1, device_id={"comp": (me_c + r) % NC, "lat": me_l}, device_id_type=pl.DeviceIdType.MESH
        )
        return carry

    def greet_lat(r, carry):
        pl.semaphore_signal(
            barrier, inc=1, device_id={"comp": me_c, "lat": (me_l + r) % NL}, device_id_type=pl.DeviceIdType.MESH
        )
        return carry

    lax.fori_loop(1, NC, greet_comp, 0)
    lax.fori_loop(1, NL, greet_lat, 0)

    for j in range(ND):
        trig[0, j] = jnp.float32(float(COS[j]))
        trig[1, j] = jnp.float32(float(SIN[j]))

    for load in loads:
        load.wait()
    starts = [jnp.int32(0)]
    for slab in range(NL):
        starts.append(starts[-1] + counts[slab])
    own_start = jnp.int32(0)
    for slab in range(NL):
        own_start = own_start + jnp.where(slab < me_l, counts[slab], 0)

    source = ((sub & 1) * 4 + (sub >> 1)) * NL + me_l
    block = (lane * 171) >> 12
    in_block = lane - block * BUCKET
    block_masks = [block == b for b in range(FOLD)]
    turns = [None] + [
        jnp.where(lane >= BUCKET * k, lane - BUCKET * k, lane - BUCKET * k + BUCKET * FOLD) & 127
        for k in range(1, FOLD)
    ]
    for v in range(TILES):
        base = jnp.full((8, 128), starts[min(FOLD * v, NL - 1)], jnp.int32)
        for b in range(1, FOLD):
            if FOLD * v + b < NL:
                base = jnp.where(block == b, starts[FOLD * v + b], base)
        pack_at[v] = ((base - source + 255) >> 8) + in_block

    for t in range(8):
        columns = pl.ds(128 * t, 128)
        spd[pl.ds(t, 8, stride=8), :] = speed[0, :, columns]
        trn[pl.ds(t, 8, stride=8), :] = turn[0, :, columns]
        msk[pl.ds(t, 8, stride=8), :] = mask[:, columns].astype(jnp.float32)

    for u in range(6):
        point = source + (lane + 128 * u) * 256
        slab = jnp.zeros((8, 128), jnp.int32)
        begin = jnp.zeros((8, 128), jnp.int32)
        for s in range(1, NL + 1):
            past = point >= starts[s]
            slab = jnp.where(past, s, slab)
            begin = jnp.where(past, starts[s], begin)
        nth = lane + 128 * u - ((begin - source + 255) >> 8)
        tile = (slab * 205) >> 10
        put_at[u] = ((slab - tile * FOLD) * BUCKET + nth) & 127
        put_tile[u] = jnp.where(slab < NL, tile, -1)

    ones = jnp.ones((128, 128), jnp.bfloat16)
    deep = lax.broadcasted_iota(jnp.int32, (128, 128), 0)
    wide = lax.broadcasted_iota(jnp.int32, (128, 128), 1)
    before = jnp.where(deep < wide, 1.0, 0.0).astype(jnp.bfloat16)
    above = jnp.where(wide < deep, 1.0, 0.0).astype(jnp.bfloat16)[:64, :64]
    sea = msk[...].astype(jnp.bfloat16)
    inside = jnp.dot(sea, before, preferred_element_type=jnp.float32)
    totals = jnp.dot(sea, ones, preferred_element_type=jnp.float32)
    offsets = jnp.dot(above, totals.astype(jnp.bfloat16), preferred_element_type=jnp.float32)
    inside = inside.astype(jnp.int32)
    offsets = offsets.astype(jnp.int32)
    low_source = (lane & 3) * NL + (lane >> 2)
    for v in range(ROWS):
        offset = offsets[8 * v : 8 * v + 8]
        point = offset + inside[8 * v : 8 * v + 8] + own_start
        lane_at[v] = ((point & 31) << 2) | ((point >> 5) & 3)
        point = offset + ((low_source - own_start - offset) & 127)
        row_at[v] = (point >> 8) & 7
        row_tile[v] = ((point >> 11) << 1) + (((point + own_start) >> 7) & 1)
    cell_at = []
    for u in range(3):
        even = cells[pl.ds(16 * u, 8, stride=2), :]
        odd = cells[pl.ds(16 * u + 1, 8, stride=2), :]
        for h in range(2):
            rho = (low_source + 128 * h - own_start) & 255
            cell = jnp.where(rho < 128, lanes(even, rho & 127), lanes(odd, rho & 127))
            cell_at.append(cell)
            back_row[u, h] = (cell >> 7) & 7
            back_tile[u, h] = cell >> 10
    for v in range(ROWS):
        index = row_at[v]
        which = row_tile[v]
        value = jnp.zeros((8, 128), jnp.int32)
        for u in POINT_TILES[v]:
            for h in range(2):
                value = jnp.where(which == 2 * u + h, sublanes(cell_at[2 * u + h], index), value)
        take_at[v] = value & 127

    for v in range(ROWS):
        rows = pl.ds(8 * v, 8)
        s = spd[rows, :]
        m = msk[rows, :]

        def eastward(x):
            east = lanes(x, (lane + 1) & 127)
            return jnp.where(lane == 127, sublanes(east, (sub + 1) & 7), east)

        face = 0.5 * (s + eastward(s)) * m * eastward(m)
        sx[v] = jnp.where((lane == 127) & (sub == 7), 0.0, face)
        trn[rows, :] = trn[rows, :] * m
        if v < ROWS - 1:
            after = pl.ds(8 * v + 8, 8)
            sy[v + 1] = 0.5 * (s + spd[after, :]) * m * msk[after, :]
    pl.semaphore_wait(barrier, NC - 1 + NL - 1)

    def first_wait(g, sem):
        ref = a_buf.at[chunk(g), pl.ds(0, NC - 1), :]
        return pltpu.make_async_copy(ref, ref, sem.at[g])

    def first_copy(g, r):
        peer = (me_c + r) % NC
        source_ref, target_ref = first_ends(g, peer)
        return pltpu.make_async_remote_copy(
            src_ref=source_ref,
            dst_ref=target_ref,
            send_sem=first_send.at[g],
            recv_sem=first_recv.at[g],
            device_id={"comp": peer, "lat": me_l},
            device_id_type=pl.DeviceIdType.MESH,
        )

    for g in (TILES,) + tuple(range(TILES)):
        for r in range(1, NC):
            first_copy(g, r).start()

    north = {"comp": me_c, "lat": (me_l + 1) % NL}
    south = {"comp": me_c, "lat": (me_l + NL - 1) % NL}

    def stat_copy(k):
        ref = (spd, msk)[k % 2]
        row = 56 if k < 2 else 0
        return pltpu.make_async_remote_copy(
            src_ref=ref.at[pl.ds(row, 8), :],
            dst_ref=stat_halo.at[k],
            send_sem=stat_send.at[k],
            recv_sem=stat_recv.at[k],
            device_id=north if k < 2 else south,
            device_id_type=pl.DeviceIdType.MESH,
        )

    for k in range(4):
        stat_copy(k).start()

    for k in range(4):
        stat_copy(k).wait()
    south_mask = jnp.where(me_l > 0, stat_halo[1], 0.0)
    north_mask = jnp.where(me_l < NL - 1, stat_halo[3], 0.0)
    sy[0] = 0.5 * (stat_halo[0] + spd[0:8, :]) * south_mask * msk[0:8, :]
    sy[8] = 0.5 * (stat_halo[2] + spd[56:64, :]) * north_mask * msk[56:64, :]

    def a_rows(direction):
        return [a_buf[direction, :, pl.ds(128 * u, 128)] for u in range(6)]

    def windows(direction, v, rows):
        at = pack_at[v]
        low = at & 127
        value = None
        for u in SLOT_TILES[v]:
            got = lanes(rows[u], low)
            value = got if value is None else jnp.where((at >> 7) == u, got, value)
        return value

    def second_copy(tile, r):
        peer = (me_l + r) % NL
        return pltpu.make_async_remote_copy(
            src_ref=m_buf.at[peer, tile],
            dst_ref=r_buf.at[tile, me_l],
            send_sem=second_send.at[tile],
            recv_sem=second_recv.at[tile],
            device_id={"comp": me_c, "lat": peer},
            device_id_type=pl.DeviceIdType.MESH,
        )

    def second_local(tile):
        return pltpu.make_async_copy(m_buf.at[me_l, tile], r_buf.at[tile, me_l], second_own.at[tile])

    def many(ref, tile, sem):
        part = ref.at[tile, pl.ds(0, NL - 1)]
        return pltpu.make_async_copy(part, part, sem.at[tile])

    def pack_tile(tile, carry):
        arrived(tile)
        rows = [a_rows(FOLD * tile + s) for s in range(FOLD)]
        octet = jnp.minimum(tile, 2) * 8
        for v in range(TILES):
            parts = [windows(FOLD * tile + s, v, rows[s]) for s in range(FOLD)]
            spare = w_last[v]
            for b, value in enumerate(swap_blocks(parts, block_masks, turns)):
                if FOLD * v + b < NL:
                    extra = lanes(spare, BUCKET * b + octet + (lane & 7))
                    m_buf[FOLD * v + b, tile] = jnp.where(lane >= 120, extra, value)
        for r in range(1, NL):
            second_copy(tile, r).start()
        second_local(tile).start()
        return carry

    def arrived(g):
        first_wait(g, first_recv).wait()
        first_local(g).wait()

    arrived(TILES)
    rows = a_rows(LAST)
    for v in range(TILES):
        w_last[v] = windows(LAST, v, rows)
    lax.fori_loop(0, TILES, pack_tile, 0)

    r_rows = r_buf.reshape(TILES, NL * 8, 128)

    def turn_points(tile, carry):
        many(r_buf, tile, second_recv).wait()
        second_local(tile).wait()
        for h in range(2):
            p_buf[tile, h] = r_rows[tile, pl.ds(h, 128, stride=2), :].T
        return carry

    lax.fori_loop(0, TILES, turn_points, 0)

    def point_rows(tile, s, u, h):
        if s is None:
            return p_buf[u, h, 120:128, :]
        return p_buf[tile, h, BUCKET * s + 8 * u : BUCKET * s + 8 * u + 8, :]

    def place(direction, tile, s):
        held = {(u, h): point_rows(tile, s, u, h) for u in range(3) for h in range(2)}
        cosine = trig[0, direction]
        sign = jnp.where(cosine >= 0.0, 1, -1)
        for v in range(ROWS):
            index = row_at[v]
            which = row_tile[v]
            value = None
            for u in POINT_TILES[v]:
                for h in range(2):
                    got = sublanes(held[u, h], index)
                    value = got if value is None else jnp.where(which == 2 * u + h, got, value)
            q = jnp.where(msk[pl.ds(8 * v, 8), :] > 0.0, lanes(value, lane_at[v]), 0.0)
            x_ext[0, direction, v + 2] = sweep_x(q, cosine * sx[v], sign, sub, lane)

    def place_tile(tile, carry):
        for s in range(FOLD):
            place(FOLD * tile + s, tile, s)
        return carry

    lax.fori_loop(0, TILES, place_tile, 0)
    place(LAST, None, None)

    def halo_copy(step, k):
        positive = pl.ds(0, SIN_POS)
        negative = pl.ds(SIN_POS, ND - SIN_POS)
        which, source_rows, target_rows, peer = (
            (positive, pl.ds(8, 2), pl.ds(0, 2), north),
            (negative, pl.ds(9, 1), pl.ds(1, 1), north),
            (positive, pl.ds(2, 1), pl.ds(10, 1), south),
            (negative, pl.ds(2, 2), pl.ds(10, 2), south),
        )[k]
        return pltpu.make_async_remote_copy(
            src_ref=x_ext.at[step, which, source_rows],
            dst_ref=x_ext.at[step, which, target_rows],
            send_sem=halo_send.at[step, k],
            recv_sem=halo_recv.at[step, k],
            device_id=peer,
            device_id_type=pl.DeviceIdType.MESH,
        )

    def sweep_y(step, positive, row_list):
        def body(direction, carry):
            sine = trig[1, direction]

            def row(r):
                value = x_ext[step, direction, r + 2]
                if r < 0:
                    value = jnp.where(me_l > 0, value, 0.0)
                if r >= ROWS:
                    value = jnp.where(me_l < NL - 1, value, 0.0)
                return value

            diffs = {}
            fluxes = {}

            def diff(f):
                if f not in diffs:
                    diffs[f] = row(f) - row(f - 1)
                return diffs[f]

            def face(f):
                if f not in fluxes:
                    if positive:
                        curvature = diff(f) - diff(f - 1)
                    else:
                        curvature = diff(f + 1) - diff(f)
                    fluxes[f] = flux(row(f - 1), diff(f), curvature, sine * sy[f])
                return fluxes[f]

            for r in row_list:
                y_buf[direction, r] = row(r) - (face(r + 1) - face(r))
            return carry

        if positive:
            lax.fori_loop(0, SIN_POS, body, 0)
        else:
            lax.fori_loop(SIN_POS, ND, body, 0)

    def sweep_theta(step, r):
        t = trn[pl.ds(pl.multiple_of(8 * r, 8), 8), :]
        forward = t >= 0.0
        q = [y_buf[j, r] for j in range(ND)]
        d = [q[(j + 1) % ND] - q[j] for j in range(ND)]

        def face(j):
            ahead = d[(j + 1) % ND] - d[j]
            behind = d[j] - d[j - 1]
            if TURN[j] >= 0:
                curvature = jnp.where(forward, behind, ahead)
            else:
                curvature = jnp.where(forward, ahead, behind)
            return flux(q[j], d[j], curvature, float(TURN[j]) * t)

        last = face(ND - 1)
        prior = last
        for j in range(ND):
            f = last if j == ND - 1 else face(j)
            value = q[j] - (f - prior)
            prior = f
            if step == 0:
                sign = 1 if COS[j] >= 0 else -1
                x_ext[1, j, r + 2] = sweep_x(value, float(COS[j]) * sx[r], sign, sub, lane)
            else:
                y_buf[j, r] = value

    inner = tuple(range(2, 6))
    outer = (0, 1, 6, 7)
    for step in range(2):
        for k in range(4):
            halo_copy(step, k).start()
        sweep_y(step, True, inner)
        sweep_y(step, False, inner)

        def inner_rows(r, carry, step=step):
            sweep_theta(step, r)
            return carry

        def outer_rows(k, carry, step=step):
            sweep_theta(step, k + 4 * (k // 2))
            return carry

        lax.fori_loop(2, 6, inner_rows, 0)
        for k in range(4):
            halo_copy(step, k).wait()
        sweep_y(step, True, outer)
        sweep_y(step, False, outer)
        lax.fori_loop(0, 4, outer_rows, 0)

    def collect(direction, tile, s):
        taken = [lanes(y_buf[direction, v], take_at[v]) for v in range(ROWS)]
        for u in range(3):
            for h in range(2):
                index = back_row[u, h]
                which = back_tile[u, h]
                value = None
                for v in ROW_TILES[u]:
                    got = sublanes(taken[v], index)
                    value = got if value is None else jnp.where(which == v, got, value)
                if s is None:
                    p_buf[u, h, 120:128, :] = value
                else:
                    p_buf[tile, h, BUCKET * s + 8 * u : BUCKET * s + 8 * u + 8, :] = value

    def third_copy(tile, r):
        peer = (me_l + r) % NL
        return pltpu.make_async_remote_copy(
            src_ref=m_buf.at[peer, tile],
            dst_ref=n_buf.at[tile, me_l],
            send_sem=third_send.at[tile],
            recv_sem=third_recv.at[tile],
            device_id={"comp": me_c, "lat": peer},
            device_id_type=pl.DeviceIdType.MESH,
        )

    def third_local(tile):
        return pltpu.make_async_copy(m_buf.at[me_l, tile], n_buf.at[tile, me_l], third_own.at[tile])

    for tile in range(TILES):
        many(r_buf, tile, second_send).wait()

    def turn_out(tile, carry):
        for h in range(2):
            r_rows[tile, pl.ds(h, 128, stride=2), :] = p_buf[tile, h].T
        for l in range(NL):
            m_buf[l, tile] = r_buf[tile, l]
        return carry

    def collect_tile(tile, carry):
        for s in range(FOLD):
            collect(FOLD * tile + s, tile, s)
        turn_out(tile, 0)
        for r in range(1, NL):
            third_copy(tile, r).start()
        third_local(tile).start()
        return carry

    collect(LAST, None, None)
    lax.fori_loop(0, TILES, collect_tile, 0)

    def put(direction, parts):
        for u in range(6):
            at = put_at[u]
            which = put_tile[u]
            value = jnp.zeros((8, 128), jnp.float32)
            for v in range(TILES):
                if u in SLOT_TILES[v]:
                    value = jnp.where(which == v, lanes(parts[v], at), value)
            o_buf[direction, :, pl.ds(128 * u, 128)] = value

    def fourth_ends(k, peer):
        part = chunk(k)
        return o_buf.at[part, slot_of(peer), :], out.at[part, me_c, :]

    def fourth_copy(k, r):
        peer = (me_c + r) % NC
        source_ref, target_ref = fourth_ends(k, peer)
        return pltpu.make_async_remote_copy(
            src_ref=source_ref,
            dst_ref=target_ref,
            send_sem=fourth_send.at[k],
            recv_sem=fourth_recv.at[k],
            device_id={"comp": peer, "lat": me_l},
            device_id_type=pl.DeviceIdType.MESH,
        )

    def fourth_local(k):
        source_ref, target_ref = fourth_ends(k, me_c)
        return pltpu.make_async_copy(source_ref, target_ref, fourth_own.at[k])

    def fourth_send_all(k):
        for r in range(1, NC):
            fourth_copy(k, r).start()
        fourth_local(k).start()

    def put_tile_of(tile, carry):
        many(n_buf, tile, third_recv).wait()
        third_local(tile).wait()
        swapped = []
        for v in range(TILES):
            parts = [n_buf[tile, min(FOLD * v + b, NL - 1)] for b in range(FOLD)]
            swapped.append(swap_blocks(parts, block_masks, turns))
        for s in range(FOLD):
            put(FOLD * tile + s, [swapped[v][s] for v in range(TILES)])
        fourth_send_all(tile)
        return carry

    def put_last():
        parts = []
        spare = 120 + (lane & 7)
        for v in range(TILES):
            value = jnp.zeros((8, 128), jnp.float32)
            for b in range(FOLD):
                if FOLD * v + b < NL:
                    for e in range(3):
                        got = lanes(n_buf[e, FOLD * v + b], spare)
                        value = jnp.where((lane >> 3) == 3 * b + e, got, value)
            parts.append(value)
        put(LAST, parts)

    lax.fori_loop(0, 3, put_tile_of, 0)
    put_last()
    fourth_send_all(TILES)
    lax.fori_loop(3, TILES, put_tile_of, 0)

    for g in range(TILES + 1):
        first_wait(g, first_send).wait()
    for tile in range(TILES):
        many(n_buf, tile, third_send).wait()
    for k in range(TILES + 1):
        fourth_local(k).wait()
        part = out.at[chunk(k), pl.ds(0, NC - 1), :]
        pltpu.make_async_copy(part, part, fourth_recv.at[k]).wait()
        pltpu.make_async_copy(part, part, fourth_send.at[k]).wait()


def per_device(spectra_in, group_speed, turn_rate, sea_mask, sea_cell, slab_counts):
    f32 = jnp.float32
    vreg = (8, 128)
    dma = pltpu.SemaphoreType.DMA
    hbm = pl.BlockSpec(memory_space=pltpu.HBM)
    anywhere = pl.BlockSpec(memory_space=pl.ANY)
    return pl.pallas_call(
        kernel,
        out_shape=jax.ShapeDtypeStruct((ND, NC, SLOTS), f32),
        in_specs=[hbm] * 6,
        out_specs=anywhere,
        scratch_shapes=[
            pltpu.VMEM((1, ROWS, 1024), f32),
            pltpu.VMEM((1, ROWS, 1024), f32),
            pltpu.VMEM((ROWS, 1024), jnp.int32),
            pltpu.VMEM((48, 128), jnp.int32),
            pltpu.SMEM((NL,), jnp.int32),
            pltpu.SMEM((2, ND), f32),
            dma((5,)),
            pltpu.VMEM((ND, NC, SLOTS), f32),
            pltpu.VMEM((NL, TILES) + vreg, f32),
            pltpu.VMEM((TILES, NL) + vreg, f32),
            pltpu.VMEM((TILES, 2, 128, 128), f32),
            pltpu.VMEM((TILES, NL) + vreg, f32),
            pltpu.VMEM((ND, NC, SLOTS), f32),
            pltpu.VMEM((2, ND, ROWS + 4) + vreg, f32),
            pltpu.VMEM((ND, ROWS) + vreg, f32),
            pltpu.VMEM((64, 128), f32),
            pltpu.VMEM((64, 128), f32),
            pltpu.VMEM((64, 128), f32),
            pltpu.VMEM((4,) + vreg, f32),
            pltpu.VMEM((ROWS,) + vreg, f32),
            pltpu.VMEM((ROWS + 1,) + vreg, f32),
            pltpu.VMEM((TILES,) + vreg, jnp.int32),
            pltpu.VMEM((6,) + vreg, jnp.int32),
            pltpu.VMEM((6,) + vreg, jnp.int32),
            pltpu.VMEM((ROWS,) + vreg, jnp.int32),
            pltpu.VMEM((ROWS,) + vreg, jnp.int32),
            pltpu.VMEM((ROWS,) + vreg, jnp.int32),
            pltpu.VMEM((ROWS,) + vreg, jnp.int32),
            pltpu.VMEM((3, 2) + vreg, jnp.int32),
            pltpu.VMEM((3, 2) + vreg, jnp.int32),
            pltpu.VMEM((TILES,) + vreg, f32),
            dma((TILES + 1,)), dma((TILES + 1,)), dma((TILES + 1,)),
            dma((TILES,)), dma((TILES,)), dma((TILES,)),
            dma((4,)), dma((4,)), dma((2, 4)), dma((2, 4)),
            dma((TILES,)), dma((TILES,)), dma((TILES,)),
            dma((TILES + 1,)), dma((TILES + 1,)), dma((TILES + 1,)),
        ],
        compiler_params=pltpu.CompilerParams(
            collective_id=0, has_side_effects=True, vmem_limit_bytes=65400 * 1024
        ),
        name="wave_step",
    )(
        spectra_in.transpose(1, 0, 2),
        group_speed,
        turn_rate,
        sea_mask,
        sea_cell.reshape(48, 128),
        slab_counts,
    ).transpose(1, 0, 2)


def solution(mesh):
    in_specs = (
        P(None, None, ("comp", "lat")),
        P("comp", "lat", None),
        P("comp", "lat", None),
        P("lat", None),
        P("lat"),
        P(),
    )
    out_specs = P(None, None, ("comp", "lat"))
    return jax.shard_map(
        per_device, mesh=mesh, in_specs=in_specs, out_specs=out_specs, check_vma=False
    )
```

```python
import math

import jax
import jax.numpy as jnp
import numpy as np
from jax import lax
from jax.experimental import pallas as pl
from jax.experimental.pallas import tpu as pltpu
from jax.sharding import PartitionSpec as P

NC = 8
NL = 32
ND = 36
SLOTS = 768
BUCKET = 24
ROWS = 8
FOLD = 5
TILES = 7
LAST = ND - 1
SIN_POS = 19

ANGLES = np.arange(ND, dtype=np.float32) * np.float32(2.0 * math.pi / ND)
COS = np.cos(ANGLES).astype(np.float32)
SIN = np.sin(ANGLES).astype(np.float32)
TURN = (0.5 * (COS + np.roll(COS, -1))).astype(np.float32)
assert (SIN[:SIN_POS] >= 0).all() and (SIN[SIN_POS:] < 0).all()

SLOT_TILES = ((0,), (0, 1), (0, 1, 2), (1, 2, 3), (1, 2, 3, 4), (2, 3, 4, 5), (2, 3, 4, 5))
POINT_TILES = tuple(
    tuple(range(max(0, 4 * v - 20) // 8, min(2, (4 * v + 3) // 8) + 1)) for v in range(ROWS)
)
ROW_TILES = tuple(tuple(range(2 * u, min(7, 2 * u + 6) + 1)) for u in range(3))


def lanes(values, index):
    return jnp.take_along_axis(values, index, axis=1)


def sublanes(values, index):
    return jnp.take_along_axis(values, index, axis=0)


def iotas():
    return (
        lax.broadcasted_iota(jnp.int32, (8, 128), 0),
        lax.broadcasted_iota(jnp.int32, (8, 128), 1),
    )


def swap_blocks(parts, block_masks, turns):
    rolled = []
    for k in range(FOLD):
        diagonal = parts[(FOLD - 1 + k) % FOLD]
        for b in range(FOLD - 1):
            diagonal = jnp.where(block_masks[b], parts[(b + k) % FOLD], diagonal)
        rolled.append(diagonal if k == 0 else lanes(diagonal, turns[k]))
    outs = []
    for a in range(FOLD):
        value = rolled[(FOLD - 1 - a) % FOLD]
        for b in range(FOLD - 1):
            value = jnp.where(block_masks[b], rolled[(b - a) % FOLD], value)
        outs.append(value)
    return outs


def flux(q, d, curvature, c):
    sixth = 1.0 / 6.0
    return c * (q + (1.0 - c) * (0.5 * d - (c * sixth + sixth) * curvature))


def sweep_x(q, c, sign, sub, lane):
    east = lanes(q, (lane + 1) & 127)
    east = jnp.where(lane == 127, sublanes(east, (sub + 1) & 7), east)
    east = jnp.where((lane == 127) & (sub == 7), 0.0, east)
    d = east - q
    side = lanes(d, (lane - sign) & 127)
    edge = lane == jnp.where(sign > 0, 0, 127)
    side = jnp.where(edge, sublanes(side, (sub - sign) & 7), side)
    side = jnp.where(edge & (sub == jnp.where(sign > 0, 0, 7)), q, side)
    curvature = (d - side) * jnp.where(sign > 0, 1.0, -1.0)
    f = flux(q, d, curvature, c)
    west = lanes(f, (lane - 1) & 127)
    west = jnp.where(lane == 0, sublanes(west, (sub - 1) & 7), west)
    return q - (f - west)


def kernel(
    spectra, speed_in, turn_in, mask_in, cells_in, counts_in, out,
    speed, turn, mask, cells, counts, trig, load_sem,
    a_buf, m_buf, r_buf, p_buf, n_buf, o_buf, x_ext, y_buf,
    spd, trn, msk, stat_halo, sx, sy,
    pack_at, put_at, put_tile, row_at, row_tile, lane_at, take_at, back_row, back_tile, w_last,
    first_send, first_recv, first_own, second_send, second_recv, second_own,
    stat_send, stat_recv, halo_send, halo_recv,
    third_send, third_recv, third_own, fourth_send, fourth_recv, fourth_own,
):
    me_c = lax.axis_index("comp")
    me_l = lax.axis_index("lat")
    sub, lane = iotas()

    def slot_of(c):
        return (c % 4) * 2 + c // 4

    loads = [
        pltpu.make_async_copy(source_ref, target_ref, load_sem.at[k])
        for k, (source_ref, target_ref) in enumerate(
            ((counts_in, counts), (speed_in, speed), (turn_in, turn), (mask_in, mask), (cells_in, cells))
        )
    ]
    for load in loads:
        load.start()

    def chunk(g):
        return pl.ds(FOLD * g, 1 if isinstance(g, int) and g == TILES else FOLD)

    def first_ends(g, peer):
        return spectra.at[chunk(g), peer, :], a_buf.at[chunk(g), slot_of(me_c), :]

    def first_local(g):
        source_ref, target_ref = first_ends(g, me_c)
        return pltpu.make_async_copy(source_ref, target_ref, first_own.at[g])

    for g in range(TILES + 1):
        first_local(g).start()

    barrier = pltpu.get_barrier_semaphore()

    def greet_comp(r, carry):
        pl.semaphore_signal(
            barrier, inc=1, device_id={"comp": (me_c + r) % NC, "lat": me_l}, device_id_type=pl.DeviceIdType.MESH
        )
        return carry

    def greet_lat(r, carry):
        pl.semaphore_signal(
            barrier, inc=1, device_id={"comp": me_c, "lat": (me_l + r) % NL}, device_id_type=pl.DeviceIdType.MESH
        )
        return carry

    lax.fori_loop(1, NC, greet_comp, 0)
    lax.fori_loop(1, NL, greet_lat, 0)

    for j in range(ND):
        trig[0, j] = jnp.float32(float(COS[j]))
        trig[1, j] = jnp.float32(float(SIN[j]))

    for load in loads:
        load.wait()
    starts = [jnp.int32(0)]
    for slab in range(NL):
        starts.append(starts[-1] + counts[slab])
    own_start = jnp.int32(0)
    for slab in range(NL):
        own_start = own_start + jnp.where(slab < me_l, counts[slab], 0)

    source = ((sub & 1) * 4 + (sub >> 1)) * NL + me_l
    block = (lane * 171) >> 12
    in_block = lane - block * BUCKET
    block_masks = [block == b for b in range(FOLD)]
    turns = [None] + [
        jnp.where(lane >= BUCKET * k, lane - BUCKET * k, lane - BUCKET * k + BUCKET * FOLD) & 127
        for k in range(1, FOLD)
    ]
    for v in range(TILES):
        base = jnp.full((8, 128), starts[min(FOLD * v, NL - 1)], jnp.int32)
        for b in range(1, FOLD):
            if FOLD * v + b < NL:
                base = jnp.where(block == b, starts[FOLD * v + b], base)
        pack_at[v] = ((base - source + 255) >> 8) + in_block

    for t in range(8):
        columns = pl.ds(128 * t, 128)
        spd[pl.ds(t, 8, stride=8), :] = speed[0, :, columns]
        trn[pl.ds(t, 8, stride=8), :] = turn[0, :, columns]
        msk[pl.ds(t, 8, stride=8), :] = mask[:, columns].astype(jnp.float32)

    for u in range(6):
        point = source + (lane + 128 * u) * 256
        slab = jnp.zeros((8, 128), jnp.int32)
        begin = jnp.zeros((8, 128), jnp.int32)
        for s in range(1, NL + 1):
            past = point >= starts[s]
            slab = jnp.where(past, s, slab)
            begin = jnp.where(past, starts[s], begin)
        nth = lane + 128 * u - ((begin - source + 255) >> 8)
        tile = (slab * 205) >> 10
        put_at[u] = ((slab - tile * FOLD) * BUCKET + nth) & 127
        put_tile[u] = jnp.where(slab < NL, tile, -1)

    ones = jnp.ones((128, 128), jnp.bfloat16)
    deep = lax.broadcasted_iota(jnp.int32, (128, 128), 0)
    wide = lax.broadcasted_iota(jnp.int32, (128, 128), 1)
    before = jnp.where(deep < wide, 1.0, 0.0).astype(jnp.bfloat16)
    above = jnp.where(wide < deep, 1.0, 0.0).astype(jnp.bfloat16)[:64, :64]
    sea = msk[...].astype(jnp.bfloat16)
    inside = jnp.dot(sea, before, preferred_element_type=jnp.float32)
    totals = jnp.dot(sea, ones, preferred_element_type=jnp.float32)
    offsets = jnp.dot(above, totals.astype(jnp.bfloat16), preferred_element_type=jnp.float32)
    inside = inside.astype(jnp.int32)
    offsets = offsets.astype(jnp.int32)
    low_source = (lane & 3) * NL + (lane >> 2)
    for v in range(ROWS):
        offset = offsets[8 * v : 8 * v + 8]
        point = offset + inside[8 * v : 8 * v + 8] + own_start
        lane_at[v] = ((point & 31) << 2) | ((point >> 5) & 3)
        point = offset + ((low_source - own_start - offset) & 127)
        row_at[v] = (point >> 8) & 7
        row_tile[v] = ((point >> 11) << 1) + (((point + own_start) >> 7) & 1)
    cell_at = []
    for u in range(3):
        even = cells[pl.ds(16 * u, 8, stride=2), :]
        odd = cells[pl.ds(16 * u + 1, 8, stride=2), :]
        for h in range(2):
            rho = (low_source + 128 * h - own_start) & 255
            cell = jnp.where(rho < 128, lanes(even, rho & 127), lanes(odd, rho & 127))
            cell_at.append(cell)
            back_row[u, h] = (cell >> 7) & 7
            back_tile[u, h] = cell >> 10
    for v in range(ROWS):
        index = row_at[v]
        which = row_tile[v]
        value = jnp.zeros((8, 128), jnp.int32)
        for u in POINT_TILES[v]:
            for h in range(2):
                value = jnp.where(which == 2 * u + h, sublanes(cell_at[2 * u + h], index), value)
        take_at[v] = value & 127

    for v in range(ROWS):
        rows = pl.ds(8 * v, 8)
        s = spd[rows, :]
        m = msk[rows, :]

        def eastward(x):
            east = lanes(x, (lane + 1) & 127)
            return jnp.where(lane == 127, sublanes(east, (sub + 1) & 7), east)

        face = 0.5 * (s + eastward(s)) * m * eastward(m)
        sx[v] = jnp.where((lane == 127) & (sub == 7), 0.0, face)
        trn[rows, :] = trn[rows, :] * m
        if v < ROWS - 1:
            after = pl.ds(8 * v + 8, 8)
            sy[v + 1] = 0.5 * (s + spd[after, :]) * m * msk[after, :]
    pl.semaphore_wait(barrier, NC - 1 + NL - 1)

    def first_wait(g, sem):
        ref = a_buf.at[chunk(g), pl.ds(0, NC - 1), :]
        return pltpu.make_async_copy(ref, ref, sem.at[g])

    def first_copy(g, r):
        peer = (me_c + r) % NC
        source_ref, target_ref = first_ends(g, peer)
        return pltpu.make_async_remote_copy(
            src_ref=source_ref,
            dst_ref=target_ref,
            send_sem=first_send.at[g],
            recv_sem=first_recv.at[g],
            device_id={"comp": peer, "lat": me_l},
            device_id_type=pl.DeviceIdType.MESH,
        )

    for g in (TILES,) + tuple(range(TILES)):
        for r in range(1, NC):
            first_copy(g, r).start()

    north = {"comp": me_c, "lat": (me_l + 1) % NL}
    south = {"comp": me_c, "lat": (me_l + NL - 1) % NL}

    def stat_copy(k):
        ref = (spd, msk)[k % 2]
        row = 56 if k < 2 else 0
        return pltpu.make_async_remote_copy(
            src_ref=ref.at[pl.ds(row, 8), :],
            dst_ref=stat_halo.at[k],
            send_sem=stat_send.at[k],
            recv_sem=stat_recv.at[k],
            device_id=north if k < 2 else south,
            device_id_type=pl.DeviceIdType.MESH,
        )

    for k in range(4):
        stat_copy(k).start()

    def a_rows(direction):
        return [a_buf[direction, :, pl.ds(128 * u, 128)] for u in range(6)]

    def windows(direction, v, rows):
        at = pack_at[v]
        low = at & 127
        value = None
        for u in SLOT_TILES[v]:
            got = lanes(rows[u], low)
            value = got if value is None else jnp.where((at >> 7) == u, got, value)
        return value

    def second_copy(tile, r):
        peer = (me_l + r) % NL
        return pltpu.make_async_remote_copy(
            src_ref=m_buf.at[peer, tile],
            dst_ref=r_buf.at[tile, me_l],
            send_sem=second_send.at[tile],
            recv_sem=second_recv.at[tile],
            device_id={"comp": me_c, "lat": peer},
            device_id_type=pl.DeviceIdType.MESH,
        )

    def second_local(tile):
        return pltpu.make_async_copy(m_buf.at[me_l, tile], r_buf.at[tile, me_l], second_own.at[tile])

    def many(ref, tile, sem):
        part = ref.at[tile, pl.ds(0, NL - 1)]
        return pltpu.make_async_copy(part, part, sem.at[tile])

    def pack_tile(tile, carry):
        arrived(tile)
        rows = [a_rows(FOLD * tile + s) for s in range(FOLD)]
        octet = jnp.minimum(tile, 2) * 8
        for v in range(TILES):
            parts = [windows(FOLD * tile + s, v, rows[s]) for s in range(FOLD)]
            spare = w_last[v]
            for b, value in enumerate(swap_blocks(parts, block_masks, turns)):
                if FOLD * v + b < NL:
                    extra = lanes(spare, BUCKET * b + octet + (lane & 7))
                    m_buf[FOLD * v + b, tile] = jnp.where(lane >= 120, extra, value)
        for r in range(1, NL):
            second_copy(tile, r).start()
        second_local(tile).start()
        return carry

    def arrived(g):
        first_wait(g, first_recv).wait()
        first_local(g).wait()

    arrived(TILES)
    rows = a_rows(LAST)
    for v in range(TILES):
        w_last[v] = windows(LAST, v, rows)
    lax.fori_loop(0, TILES, pack_tile, 0)

    for k in range(4):
        stat_copy(k).wait()
    south_mask = jnp.where(me_l > 0, stat_halo[1], 0.0)
    north_mask = jnp.where(me_l < NL - 1, stat_halo[3], 0.0)
    sy[0] = 0.5 * (stat_halo[0] + spd[0:8, :]) * south_mask * msk[0:8, :]
    sy[8] = 0.5 * (stat_halo[2] + spd[56:64, :]) * north_mask * msk[56:64, :]

    r_rows = r_buf.reshape(TILES, NL * 8, 128)

    def turn_points(tile, carry):
        many(r_buf, tile, second_recv).wait()
        second_local(tile).wait()
        for h in range(2):
            p_buf[tile, h] = r_rows[tile, pl.ds(h, 128, stride=2), :].T
        return carry

    def point_rows(tile, s, u, h):
        if s is None:
            return p_buf[u, h, 120:128, :]
        return p_buf[tile, h, BUCKET * s + 8 * u : BUCKET * s + 8 * u + 8, :]

    def place(direction, tile, s):
        held = {(u, h): point_rows(tile, s, u, h) for u in range(3) for h in range(2)}
        cosine = trig[0, direction]
        sign = jnp.where(cosine >= 0.0, 1, -1)
        for v in range(ROWS):
            index = row_at[v]
            which = row_tile[v]
            value = None
            for u in POINT_TILES[v]:
                for h in range(2):
                    got = sublanes(held[u, h], index)
                    value = got if value is None else jnp.where(which == 2 * u + h, got, value)
            q = jnp.where(msk[pl.ds(8 * v, 8), :] > 0.0, lanes(value, lane_at[v]), 0.0)
            x_ext[0, direction, v + 2] = sweep_x(q, cosine * sx[v], sign, sub, lane)

    def halo_copy(step, dirs, rows, to_north, k):
        source_row = 2 + ROWS - rows if to_north else 2
        target_row = 2 - rows if to_north else 2 + ROWS
        return pltpu.make_async_remote_copy(
            src_ref=x_ext.at[step, dirs, pl.ds(source_row, rows)],
            dst_ref=x_ext.at[step, dirs, pl.ds(target_row, rows)],
            send_sem=halo_send.at[step, k],
            recv_sem=halo_recv.at[step, k],
            device_id=north if to_north else south,
            device_id_type=pl.DeviceIdType.MESH,
        )

    def tile_halos(tile, kind):
        north_rows, south_rows = ((2, 1), (2, 2), (1, 2))[kind]
        dirs = pl.ds(FOLD * tile, 1 if isinstance(tile, int) and tile == TILES else FOLD)
        return (
            halo_copy(0, dirs, north_rows, True, 2 * tile),
            halo_copy(0, dirs, south_rows, False, 2 * tile + 1),
        )

    def second_halos():
        positive = pl.ds(0, SIN_POS)
        negative = pl.ds(SIN_POS, ND - SIN_POS)
        return (
            halo_copy(1, positive, 2, True, 0),
            halo_copy(1, negative, 1, True, 1),
            halo_copy(1, positive, 1, False, 2),
            halo_copy(1, negative, 2, False, 3),
        )

    def sweep_y(step, direction, positive, row_list):
        sine = trig[1, direction]

        def row(r):
            value = x_ext[step, direction, r + 2]
            if r < 0:
                value = jnp.where(me_l > 0, value, 0.0)
            if r >= ROWS:
                value = jnp.where(me_l < NL - 1, value, 0.0)
            return value

        diffs = {}
        fluxes = {}

        def diff(f):
            if f not in diffs:
                diffs[f] = row(f) - row(f - 1)
            return diffs[f]

        def face(f):
            if f not in fluxes:
                if positive:
                    curvature = diff(f) - diff(f - 1)
                else:
                    curvature = diff(f + 1) - diff(f)
                fluxes[f] = flux(row(f - 1), diff(f), curvature, sine * sy[f])
            return fluxes[f]

        for r in row_list:
            y_buf[direction, r] = row(r) - (face(r + 1) - face(r))

    def sweep_y_all(step, row_list):
        def body(positive):
            def one(direction, carry):
                sweep_y(step, direction, positive, row_list)
                return carry

            return one

        lax.fori_loop(0, SIN_POS, body(True), 0)
        lax.fori_loop(SIN_POS, ND, body(False), 0)

    inner = tuple(range(2, 6))
    outer = (0, 1, 6, 7)

    def receive_tile(kind):
        def body(tile, carry):
            turn_points(tile, 0)
            for s in range(FOLD):
                place(FOLD * tile + s, tile, s)
            for copy in tile_halos(tile, kind):
                copy.start()
            for s in range(FOLD):
                positive = kind == 0 or (kind == 1 and FOLD * tile + s < SIN_POS)
                sweep_y(0, FOLD * tile + s, positive, inner)
            return carry

        return body

    middle = SIN_POS // FOLD
    lax.fori_loop(0, middle, receive_tile(0), 0)
    place(LAST, None, None)
    for copy in tile_halos(TILES, 2):
        copy.start()
    sweep_y(0, LAST, False, inner)
    receive_tile(1)(middle, 0)
    lax.fori_loop(middle + 1, TILES, receive_tile(2), 0)

    def sweep_theta(step, r):
        t = trn[pl.ds(pl.multiple_of(8 * r, 8), 8), :]
        forward = t >= 0.0
        q = [y_buf[j, r] for j in range(ND)]
        d = [q[(j + 1) % ND] - q[j] for j in range(ND)]

        def face(j):
            ahead = d[(j + 1) % ND] - d[j]
            behind = d[j] - d[j - 1]
            if TURN[j] >= 0:
                curvature = jnp.where(forward, behind, ahead)
            else:
                curvature = jnp.where(forward, ahead, behind)
            return flux(q[j], d[j], curvature, float(TURN[j]) * t)

        last = face(ND - 1)
        prior = last
        for j in range(ND):
            f = last if j == ND - 1 else face(j)
            value = q[j] - (f - prior)
            prior = f
            if step == 0:
                sign = 1 if COS[j] >= 0 else -1
                x_ext[1, j, r + 2] = sweep_x(value, float(COS[j]) * sx[r], sign, sub, lane)
            else:
                y_buf[j, r] = value

    def theta_inner(step):
        def body(r, carry):
            sweep_theta(step, r)
            return carry

        lax.fori_loop(2, 6, body, 0)

    def theta_outer(step):
        def body(k, carry):
            sweep_theta(step, k + 4 * (k // 2))
            return carry

        lax.fori_loop(0, 4, body, 0)

    theta_inner(0)
    for tile in range(TILES + 1):
        for copy in tile_halos(tile, 0 if tile < middle else 1 if tile == middle else 2):
            copy.wait()
    sweep_y_all(0, outer)
    theta_outer(0)
    for copy in second_halos():
        copy.start()
    sweep_y_all(1, inner)
    theta_inner(1)
    for copy in second_halos():
        copy.wait()
    sweep_y_all(1, outer)
    theta_outer(1)

    def collect(direction, tile, s):
        taken = [lanes(y_buf[direction, v], take_at[v]) for v in range(ROWS)]
        for u in range(3):
            for h in range(2):
                index = back_row[u, h]
                which = back_tile[u, h]
                value = None
                for v in ROW_TILES[u]:
                    got = sublanes(taken[v], index)
                    value = got if value is None else jnp.where(which == v, got, value)
                if s is None:
                    p_buf[u, h, 120:128, :] = value
                else:
                    p_buf[tile, h, BUCKET * s + 8 * u : BUCKET * s + 8 * u + 8, :] = value

    def third_copy(tile, r):
        peer = (me_l + r) % NL
        return pltpu.make_async_remote_copy(
            src_ref=m_buf.at[peer, tile],
            dst_ref=n_buf.at[tile, me_l],
            send_sem=third_send.at[tile],
            recv_sem=third_recv.at[tile],
            device_id={"comp": me_c, "lat": peer},
            device_id_type=pl.DeviceIdType.MESH,
        )

    def third_local(tile):
        return pltpu.make_async_copy(m_buf.at[me_l, tile], n_buf.at[tile, me_l], third_own.at[tile])

    for tile in range(TILES):
        many(r_buf, tile, second_send).wait()

    def turn_out(tile, carry):
        for h in range(2):
            r_rows[tile, pl.ds(h, 128, stride=2), :] = p_buf[tile, h].T
        for l in range(NL):
            m_buf[l, tile] = r_buf[tile, l]
        return carry

    def collect_tile(tile, carry):
        for s in range(FOLD):
            collect(FOLD * tile + s, tile, s)
        turn_out(tile, 0)
        for r in range(1, NL):
            third_copy(tile, r).start()
        third_local(tile).start()
        return carry

    collect(LAST, None, None)
    lax.fori_loop(0, TILES, collect_tile, 0)

    def put(direction, parts):
        for u in range(6):
            at = put_at[u]
            which = put_tile[u]
            value = jnp.zeros((8, 128), jnp.float32)
            for v in range(TILES):
                if u in SLOT_TILES[v]:
                    value = jnp.where(which == v, lanes(parts[v], at), value)
            o_buf[direction, :, pl.ds(128 * u, 128)] = value

    def fourth_ends(k, peer):
        part = chunk(k)
        return o_buf.at[part, slot_of(peer), :], out.at[part, me_c, :]

    def fourth_copy(k, r):
        peer = (me_c + r) % NC
        source_ref, target_ref = fourth_ends(k, peer)
        return pltpu.make_async_remote_copy(
            src_ref=source_ref,
            dst_ref=target_ref,
            send_sem=fourth_send.at[k],
            recv_sem=fourth_recv.at[k],
            device_id={"comp": peer, "lat": me_l},
            device_id_type=pl.DeviceIdType.MESH,
        )

    def fourth_local(k):
        source_ref, target_ref = fourth_ends(k, me_c)
        return pltpu.make_async_copy(source_ref, target_ref, fourth_own.at[k])

    def fourth_send_all(k):
        for r in range(1, NC):
            fourth_copy(k, r).start()
        fourth_local(k).start()

    def put_tile_of(tile, carry):
        many(n_buf, tile, third_recv).wait()
        third_local(tile).wait()
        swapped = []
        for v in range(TILES):
            parts = [n_buf[tile, min(FOLD * v + b, NL - 1)] for b in range(FOLD)]
            swapped.append(swap_blocks(parts, block_masks, turns))
        for s in range(FOLD):
            put(FOLD * tile + s, [swapped[v][s] for v in range(TILES)])
        fourth_send_all(tile)
        return carry

    def put_last():
        parts = []
        spare = 120 + (lane & 7)
        for v in range(TILES):
            value = jnp.zeros((8, 128), jnp.float32)
            for b in range(FOLD):
                if FOLD * v + b < NL:
                    for e in range(3):
                        got = lanes(n_buf[e, FOLD * v + b], spare)
                        value = jnp.where((lane >> 3) == 3 * b + e, got, value)
            parts.append(value)
        put(LAST, parts)

    lax.fori_loop(0, 3, put_tile_of, 0)
    put_last()
    fourth_send_all(TILES)
    lax.fori_loop(3, TILES, put_tile_of, 0)

    for g in range(TILES + 1):
        first_wait(g, first_send).wait()
    for tile in range(TILES):
        many(n_buf, tile, third_send).wait()
    for k in range(TILES + 1):
        fourth_local(k).wait()
        part = out.at[chunk(k), pl.ds(0, NC - 1), :]
        pltpu.make_async_copy(part, part, fourth_recv.at[k]).wait()
        pltpu.make_async_copy(part, part, fourth_send.at[k]).wait()


def per_device(spectra_in, group_speed, turn_rate, sea_mask, sea_cell, slab_counts):
    f32 = jnp.float32
    vreg = (8, 128)
    dma = pltpu.SemaphoreType.DMA
    hbm = pl.BlockSpec(memory_space=pltpu.HBM)
    anywhere = pl.BlockSpec(memory_space=pl.ANY)
    return pl.pallas_call(
        kernel,
        out_shape=pltpu.VMEM((ND, NC, SLOTS), f32),
        in_specs=[hbm] * 6,
        out_specs=anywhere,
        scratch_shapes=[
            pltpu.VMEM((1, ROWS, 1024), f32),
            pltpu.VMEM((1, ROWS, 1024), f32),
            pltpu.VMEM((ROWS, 1024), jnp.int32),
            pltpu.VMEM((48, 128), jnp.int32),
            pltpu.SMEM((NL,), jnp.int32),
            pltpu.SMEM((2, ND), f32),
            dma((5,)),
            pltpu.VMEM((ND, NC, SLOTS), f32),
            pltpu.VMEM((NL, TILES) + vreg, f32),
            pltpu.VMEM((TILES, NL) + vreg, f32),
            pltpu.VMEM((TILES, 2, 128, 128), f32),
            pltpu.VMEM((TILES, NL) + vreg, f32),
            pltpu.VMEM((ND, NC, SLOTS), f32),
            pltpu.VMEM((2, ND, ROWS + 4) + vreg, f32),
            pltpu.VMEM((ND, ROWS) + vreg, f32),
            pltpu.VMEM((64, 128), f32),
            pltpu.VMEM((64, 128), f32),
            pltpu.VMEM((64, 128), f32),
            pltpu.VMEM((4,) + vreg, f32),
            pltpu.VMEM((ROWS,) + vreg, f32),
            pltpu.VMEM((ROWS + 1,) + vreg, f32),
            pltpu.VMEM((TILES,) + vreg, jnp.int32),
            pltpu.VMEM((6,) + vreg, jnp.int32),
            pltpu.VMEM((6,) + vreg, jnp.int32),
            pltpu.VMEM((ROWS,) + vreg, jnp.int32),
            pltpu.VMEM((ROWS,) + vreg, jnp.int32),
            pltpu.VMEM((ROWS,) + vreg, jnp.int32),
            pltpu.VMEM((ROWS,) + vreg, jnp.int32),
            pltpu.VMEM((3, 2) + vreg, jnp.int32),
            pltpu.VMEM((3, 2) + vreg, jnp.int32),
            pltpu.VMEM((TILES,) + vreg, f32),
            dma((TILES + 1,)), dma((TILES + 1,)), dma((TILES + 1,)),
            dma((TILES,)), dma((TILES,)), dma((TILES,)),
            dma((4,)), dma((4,)), dma((2, 2 * TILES + 2)), dma((2, 2 * TILES + 2)),
            dma((TILES,)), dma((TILES,)), dma((TILES,)),
            dma((TILES + 1,)), dma((TILES + 1,)), dma((TILES + 1,)),
        ],
        compiler_params=pltpu.CompilerParams(
            collective_id=0, has_side_effects=True, vmem_limit_bytes=64000 * 1024
        ),
        name="wave_step",
    )(
        spectra_in.transpose(1, 0, 2),
        group_speed,
        turn_rate,
        sea_mask,
        sea_cell.reshape(48, 128),
        slab_counts,
    ).transpose(1, 0, 2)


def solution(mesh):
    in_specs = (
        P(None, None, ("comp", "lat")),
        P("comp", "lat", None),
        P("comp", "lat", None),
        P("lat", None),
        P("lat"),
        P(),
    )
    out_specs = P(None, None, ("comp", "lat"))
    return jax.shard_map(
        per_device, mesh=mesh, in_specs=in_specs, out_specs=out_specs, check_vma=False
    )
```

```python
import math

import jax
import jax.numpy as jnp
import numpy as np
from jax import lax
from jax.experimental import pallas as pl
from jax.experimental.pallas import tpu as pltpu
from jax.sharding import PartitionSpec as P

NC = 8
NL = 32
ND = 36
SLOTS = 768
BUCKET = 24
ROWS = 8
FOLD = 5
TILES = 7
EARLY = 3
LAST = ND - 1
SIN_POS = 19

ANGLES = np.arange(ND, dtype=np.float32) * np.float32(2.0 * math.pi / ND)
COS = np.cos(ANGLES).astype(np.float32)
SIN = np.sin(ANGLES).astype(np.float32)
TURN = (0.5 * (COS + np.roll(COS, -1))).astype(np.float32)
assert (SIN[:SIN_POS] >= 0).all() and (SIN[SIN_POS:] < 0).all()

SLOT_TILES = ((0,), (0, 1), (0, 1, 2), (1, 2, 3), (1, 2, 3, 4), (2, 3, 4, 5), (2, 3, 4, 5))
POINT_TILES = tuple(
    tuple(range(max(0, 4 * v - 20) // 8, min(2, (4 * v + 3) // 8) + 1)) for v in range(ROWS)
)
ROW_TILES = tuple(tuple(range(2 * u, min(7, 2 * u + 6) + 1)) for u in range(3))


def lanes(values, index):
    return jnp.take_along_axis(values, index, axis=1)


def sublanes(values, index):
    return jnp.take_along_axis(values, index, axis=0)


def iotas():
    return (
        lax.broadcasted_iota(jnp.int32, (8, 128), 0),
        lax.broadcasted_iota(jnp.int32, (8, 128), 1),
    )


def swap_blocks(parts, block_masks, turns):
    rolled = []
    for k in range(FOLD):
        diagonal = parts[(FOLD - 1 + k) % FOLD]
        for b in range(FOLD - 1):
            diagonal = jnp.where(block_masks[b], parts[(b + k) % FOLD], diagonal)
        rolled.append(diagonal if k == 0 else lanes(diagonal, turns[k]))
    outs = []
    for a in range(FOLD):
        value = rolled[(FOLD - 1 - a) % FOLD]
        for b in range(FOLD - 1):
            value = jnp.where(block_masks[b], rolled[(b - a) % FOLD], value)
        outs.append(value)
    return outs


def flux(q, d, curvature, c):
    sixth = 1.0 / 6.0
    return c * (q + (1.0 - c) * (0.5 * d - (c * sixth + sixth) * curvature))


def sweep_x(q, c, sign, sub, lane):
    east = lanes(q, (lane + 1) & 127)
    east = jnp.where(lane == 127, sublanes(east, (sub + 1) & 7), east)
    east = jnp.where((lane == 127) & (sub == 7), 0.0, east)
    d = east - q
    side = lanes(d, (lane - sign) & 127)
    edge = lane == jnp.where(sign > 0, 0, 127)
    side = jnp.where(edge, sublanes(side, (sub - sign) & 7), side)
    side = jnp.where(edge & (sub == jnp.where(sign > 0, 0, 7)), q, side)
    curvature = (d - side) * jnp.where(sign > 0, 1.0, -1.0)
    f = flux(q, d, curvature, c)
    west = lanes(f, (lane - 1) & 127)
    west = jnp.where(lane == 0, sublanes(west, (sub - 1) & 7), west)
    return q - (f - west)


def kernel(
    spectra, speed_in, turn_in, mask_in, cells_in, counts_in, out,
    speed, turn, mask, cells, counts, trig, load_sem,
    a_buf, own_buf, m_buf, x_buf, r_buf, p_buf, z_buf, n_buf, o_buf, x_ext, y_buf,
    spd, trn, msk, stat_halo, sx, sy,
    pack_at, own_at, put_at, put_tile, own_put_at, own_put_tile, row_at, row_tile, lane_at, take_at, back_row, back_tile, w_last,
    first_send, first_recv, first_own, second_send, second_recv, second_own,
    cross_send, cross_recv, cross_own, back_send, back_recv, back_own,
    stat_send, stat_recv, halo_send, halo_recv,
    third_send, third_recv, third_own, fourth_send, fourth_recv, fourth_own,
):
    me_c = lax.axis_index("comp")
    me_l = lax.axis_index("lat")
    sub, lane = iotas()

    def slot_of(c):
        return (c % 4) * 2 + c // 4

    loads = [
        pltpu.make_async_copy(source_ref, target_ref, load_sem.at[k])
        for k, (source_ref, target_ref) in enumerate(
            (
                (counts_in, counts),
                (spectra.at[pl.ds(0, FOLD * EARLY)], own_buf.at[pl.ds(0, FOLD * EARLY)]),
                (spectra.at[pl.ds(LAST, 1)], own_buf.at[pl.ds(LAST, 1)]),
                (speed_in, speed),
                (turn_in, turn),
                (mask_in, mask),
                (cells_in, cells),
            )
        )
    ]
    for load in loads:
        load.start()

    def chunk(tile):
        return pl.ds(FOLD * tile, FOLD)

    def first_ends(g, peer):
        return spectra.at[chunk(g), peer, :], a_buf.at[chunk(g), slot_of(me_c), :]

    def first_local(g):
        source_ref, target_ref = first_ends(g, me_c)
        return pltpu.make_async_copy(source_ref, target_ref, first_own.at[g])

    for g in range(EARLY, TILES):
        first_local(g).start()

    barrier = pltpu.get_barrier_semaphore()

    def greet_comp(r, carry):
        pl.semaphore_signal(
            barrier, inc=1, device_id={"comp": (me_c + r) % NC, "lat": me_l}, device_id_type=pl.DeviceIdType.MESH
        )
        return carry

    def greet_lat(r, carry):
        pl.semaphore_signal(
            barrier, inc=1, device_id={"comp": me_c, "lat": (me_l + r) % NL}, device_id_type=pl.DeviceIdType.MESH
        )
        return carry

    lax.fori_loop(1, NC, greet_comp, 0)
    lax.fori_loop(1, NL, greet_lat, 0)

    for j in range(ND):
        trig[0, j] = jnp.float32(float(COS[j]))
        trig[1, j] = jnp.float32(float(SIN[j]))

    for load in loads:
        load.wait()
    starts = [jnp.int32(0)]
    for slab in range(NL):
        starts.append(starts[-1] + counts[slab])
    own_start = jnp.int32(0)
    for slab in range(NL):
        own_start = own_start + jnp.where(slab < me_l, counts[slab], 0)

    source = ((sub & 1) * 4 + (sub >> 1)) * NL + me_l
    own_source = me_c * NL + me_l
    block = (lane * 171) >> 12
    in_block = lane - block * BUCKET
    block_masks = [block == b for b in range(FOLD)]
    turns = [None] + [
        jnp.where(lane >= BUCKET * k, lane - BUCKET * k, lane - BUCKET * k + BUCKET * FOLD) & 127
        for k in range(1, FOLD)
    ]
    for v in range(TILES):
        base = jnp.full((8, 128), starts[min(FOLD * v, NL - 1)], jnp.int32)
        for b in range(1, FOLD):
            if FOLD * v + b < NL:
                base = jnp.where(block == b, starts[FOLD * v + b], base)
        pack_at[v] = ((base - source + 255) >> 8) + in_block
        own_at[v] = ((base - own_source + 255) >> 8) + in_block

    for t in range(8):
        columns = pl.ds(128 * t, 128)
        spd[pl.ds(t, 8, stride=8), :] = speed[0, :, columns]
        trn[pl.ds(t, 8, stride=8), :] = turn[0, :, columns]
        msk[pl.ds(t, 8, stride=8), :] = mask[:, columns].astype(jnp.float32)

    for u in range(6):
        for origin, at, which in ((source, put_at, put_tile), (own_source, own_put_at, own_put_tile)):
            point = origin + (lane + 128 * u) * 256
            slab = jnp.zeros((8, 128), jnp.int32)
            begin = jnp.zeros((8, 128), jnp.int32)
            for s in range(1, NL + 1):
                past = point >= starts[s]
                slab = jnp.where(past, s, slab)
                begin = jnp.where(past, starts[s], begin)
            nth = lane + 128 * u - ((begin - origin + 255) >> 8)
            tile = (slab * 205) >> 10
            at[u] = ((slab - tile * FOLD) * BUCKET + nth) & 127
            which[u] = jnp.where(slab < NL, tile, -1)

    ones = jnp.ones((128, 128), jnp.bfloat16)
    deep = lax.broadcasted_iota(jnp.int32, (128, 128), 0)
    wide = lax.broadcasted_iota(jnp.int32, (128, 128), 1)
    before = jnp.where(deep < wide, 1.0, 0.0).astype(jnp.bfloat16)
    above = jnp.where(wide < deep, 1.0, 0.0).astype(jnp.bfloat16)[:64, :64]
    sea = msk[...].astype(jnp.bfloat16)
    inside = jnp.dot(sea, before, preferred_element_type=jnp.float32)
    totals = jnp.dot(sea, ones, preferred_element_type=jnp.float32)
    offsets = jnp.dot(above, totals.astype(jnp.bfloat16), preferred_element_type=jnp.float32)
    inside = inside.astype(jnp.int32)
    offsets = offsets.astype(jnp.int32)
    low_source = (lane & 3) * NL + (lane >> 2)
    for v in range(ROWS):
        offset = offsets[8 * v : 8 * v + 8]
        point = offset + inside[8 * v : 8 * v + 8] + own_start
        lane_at[v] = ((point & 31) << 2) | ((point >> 5) & 3)
        point = offset + ((low_source - own_start - offset) & 127)
        row_at[v] = (point >> 8) & 7
        row_tile[v] = ((point >> 11) << 1) + (((point + own_start) >> 7) & 1)
    cell_at = []
    for u in range(3):
        even = cells[pl.ds(16 * u, 8, stride=2), :]
        odd = cells[pl.ds(16 * u + 1, 8, stride=2), :]
        for h in range(2):
            rho = (low_source + 128 * h - own_start) & 255
            cell = jnp.where(rho < 128, lanes(even, rho & 127), lanes(odd, rho & 127))
            cell_at.append(cell)
            back_row[u, h] = (cell >> 7) & 7
            back_tile[u, h] = cell >> 10
    for v in range(ROWS):
        index = row_at[v]
        which = row_tile[v]
        value = jnp.zeros((8, 128), jnp.int32)
        for u in POINT_TILES[v]:
            for h in range(2):
                value = jnp.where(which == 2 * u + h, sublanes(cell_at[2 * u + h], index), value)
        take_at[v] = value & 127

    for v in range(ROWS):
        rows = pl.ds(8 * v, 8)
        s = spd[rows, :]
        m = msk[rows, :]

        def eastward(x):
            east = lanes(x, (lane + 1) & 127)
            return jnp.where(lane == 127, sublanes(east, (sub + 1) & 7), east)

        face = 0.5 * (s + eastward(s)) * m * eastward(m)
        sx[v] = jnp.where((lane == 127) & (sub == 7), 0.0, face)
        trn[rows, :] = trn[rows, :] * m
        if v < ROWS - 1:
            after = pl.ds(8 * v + 8, 8)
            sy[v + 1] = 0.5 * (s + spd[after, :]) * m * msk[after, :]
    pl.semaphore_wait(barrier, NC - 1 + NL - 1)

    def first_wait(g, sem):
        ref = a_buf.at[chunk(g), pl.ds(0, NC - 1), :]
        return pltpu.make_async_copy(ref, ref, sem.at[g])

    def first_copy(g, r):
        peer = (me_c + r) % NC
        source_ref, target_ref = first_ends(g, peer)
        return pltpu.make_async_remote_copy(
            src_ref=source_ref,
            dst_ref=target_ref,
            send_sem=first_send.at[g],
            recv_sem=first_recv.at[g],
            device_id={"comp": peer, "lat": me_l},
            device_id_type=pl.DeviceIdType.MESH,
        )

    for g in range(EARLY, TILES):
        for r in range(1, NC):
            first_copy(g, r).start()

    north = {"comp": me_c, "lat": (me_l + 1) % NL}
    south = {"comp": me_c, "lat": (me_l + NL - 1) % NL}

    def stat_copy(k):
        ref = (spd, msk)[k % 2]
        row = 56 if k < 2 else 0
        return pltpu.make_async_remote_copy(
            src_ref=ref.at[pl.ds(row, 8), :],
            dst_ref=stat_halo.at[k],
            send_sem=stat_send.at[k],
            recv_sem=stat_recv.at[k],
            device_id=north if k < 2 else south,
            device_id_type=pl.DeviceIdType.MESH,
        )

    for k in range(4):
        stat_copy(k).start()

    def slot_rows(buffer, direction):
        return [buffer[direction, :, pl.ds(128 * u, 128)] for u in range(6)]

    def windows(at_ref, v, rows):
        at = at_ref[v]
        low = at & 127
        value = None
        for u in SLOT_TILES[v]:
            got = lanes(rows[u], low)
            value = got if value is None else jnp.where((at >> 7) == u, got, value)
        return value

    def second_copy(tile, r, early):
        peer = (me_l + r) % NL
        return pltpu.make_async_remote_copy(
            src_ref=m_buf.at[peer, tile],
            dst_ref=x_buf.at[tile, me_l] if early else r_buf.at[tile, me_l],
            send_sem=second_send.at[tile],
            recv_sem=second_recv.at[tile],
            device_id={"comp": me_c, "lat": peer},
            device_id_type=pl.DeviceIdType.MESH,
        )

    def second_local(tile, early):
        return pltpu.make_async_copy(
            m_buf.at[me_l, tile],
            x_buf.at[tile, me_l] if early else r_buf.at[tile, me_l],
            second_own.at[tile],
        )

    def many(ref, tile, sem):
        part = ref.at[tile, pl.ds(0, NL - 1)]
        return pltpu.make_async_copy(part, part, sem.at[tile])

    def pack_tile(early):
        def body(tile, carry):
            if early:
                buffer, at_ref = own_buf, own_at
            else:
                buffer, at_ref = a_buf, pack_at
                first_wait(tile, first_recv).wait()
                first_local(tile).wait()
            rows = [slot_rows(buffer, FOLD * tile + s) for s in range(FOLD)]
            for v in range(TILES):
                parts = [windows(at_ref, v, rows[s]) for s in range(FOLD)]
                for b, value in enumerate(swap_blocks(parts, block_masks, turns)):
                    if FOLD * v + b < NL:
                        if early:
                            extra = lanes(w_last[v], BUCKET * b + 8 * tile + (lane & 7))
                            value = jnp.where(lane >= 120, extra, value)
                        m_buf[FOLD * v + b, tile] = value
            for r in range(1, NL):
                second_copy(tile, r, early).start()
            second_local(tile, early).start()
            return carry

        return body

    last_rows = slot_rows(own_buf, LAST)
    for v in range(TILES):
        w_last[v] = windows(own_at, v, last_rows)
    lax.fori_loop(0, EARLY, pack_tile(True), 0)
    lax.fori_loop(EARLY, TILES, pack_tile(False), 0)

    def cross_ends(tile, peer):
        return x_buf.at[tile, :, peer, :], r_buf.at[tile, :, slot_of(me_c), :]

    def cross_copy(tile, r):
        peer = (me_c + r) % NC
        source_ref, target_ref = cross_ends(tile, peer)
        return pltpu.make_async_remote_copy(
            src_ref=source_ref,
            dst_ref=target_ref,
            send_sem=cross_send.at[tile],
            recv_sem=cross_recv.at[tile],
            device_id={"comp": peer, "lat": me_l},
            device_id_type=pl.DeviceIdType.MESH,
        )

    def cross_local(tile):
        source_ref, target_ref = cross_ends(tile, me_c)
        return pltpu.make_async_copy(source_ref, target_ref, cross_own.at[tile])

    def cross_many(ref, tile, sem):
        part = ref.at[tile, :, pl.ds(0, NC - 1), :]
        return pltpu.make_async_copy(part, part, sem.at[tile])

    def cross_tile(tile, carry):
        many(x_buf, tile, second_recv).wait()
        second_local(tile, True).wait()
        for r in range(1, NC):
            cross_copy(tile, r).start()
        cross_local(tile).start()
        return carry

    lax.fori_loop(0, EARLY, cross_tile, 0)

    for k in range(4):
        stat_copy(k).wait()
    south_mask = jnp.where(me_l > 0, stat_halo[1], 0.0)
    north_mask = jnp.where(me_l < NL - 1, stat_halo[3], 0.0)
    sy[0] = 0.5 * (stat_halo[0] + spd[0:8, :]) * south_mask * msk[0:8, :]
    sy[8] = 0.5 * (stat_halo[2] + spd[56:64, :]) * north_mask * msk[56:64, :]

    r_rows = r_buf.reshape(TILES, NL * 8, 128)

    def turn_points(tile, early):
        if early:
            cross_many(r_buf, tile, cross_recv).wait()
            cross_local(tile).wait()
        else:
            many(r_buf, tile, second_recv).wait()
            second_local(tile, False).wait()
        for h in range(2):
            p_buf[tile, h] = r_rows[tile, pl.ds(h, 128, stride=2), :].T

    def point_rows(tile, s, u, h):
        if s is None:
            return p_buf[u, h, 120:128, :]
        return p_buf[tile, h, BUCKET * s + 8 * u : BUCKET * s + 8 * u + 8, :]

    def place(direction, tile, s):
        held = {(u, h): point_rows(tile, s, u, h) for u in range(3) for h in range(2)}
        cosine = trig[0, direction]
        sign = jnp.where(cosine >= 0.0, 1, -1)
        for v in range(ROWS):
            index = row_at[v]
            which = row_tile[v]
            value = None
            for u in POINT_TILES[v]:
                for h in range(2):
                    got = sublanes(held[u, h], index)
                    value = got if value is None else jnp.where(which == 2 * u + h, got, value)
            q = jnp.where(msk[pl.ds(8 * v, 8), :] > 0.0, lanes(value, lane_at[v]), 0.0)
            x_ext[0, direction, v + 2] = sweep_x(q, cosine * sx[v], sign, sub, lane)

    def halo_copy(step, dirs, rows, to_north, k):
        source_row = 2 + ROWS - rows if to_north else 2
        target_row = 2 - rows if to_north else 2 + ROWS
        return pltpu.make_async_remote_copy(
            src_ref=x_ext.at[step, dirs, pl.ds(source_row, rows)],
            dst_ref=x_ext.at[step, dirs, pl.ds(target_row, rows)],
            send_sem=halo_send.at[step, k],
            recv_sem=halo_recv.at[step, k],
            device_id=north if to_north else south,
            device_id_type=pl.DeviceIdType.MESH,
        )

    def tile_halos(tile, kind):
        north_rows, south_rows = ((2, 1), (2, 2), (1, 2))[kind]
        dirs = pl.ds(FOLD * tile, 1 if isinstance(tile, int) and tile == TILES else FOLD)
        return (
            halo_copy(0, dirs, north_rows, True, 2 * tile),
            halo_copy(0, dirs, south_rows, False, 2 * tile + 1),
        )

    def second_halos():
        positive = pl.ds(0, SIN_POS)
        negative = pl.ds(SIN_POS, ND - SIN_POS)
        return (
            halo_copy(1, positive, 2, True, 0),
            halo_copy(1, negative, 1, True, 1),
            halo_copy(1, positive, 1, False, 2),
            halo_copy(1, negative, 2, False, 3),
        )

    def sweep_y(step, direction, positive, row_list):
        sine = trig[1, direction]

        def row(r):
            value = x_ext[step, direction, r + 2]
            if r < 0:
                value = jnp.where(me_l > 0, value, 0.0)
            if r >= ROWS:
                value = jnp.where(me_l < NL - 1, value, 0.0)
            return value

        diffs = {}
        fluxes = {}

        def diff(f):
            if f not in diffs:
                diffs[f] = row(f) - row(f - 1)
            return diffs[f]

        def face(f):
            if f not in fluxes:
                if positive:
                    curvature = diff(f) - diff(f - 1)
                else:
                    curvature = diff(f + 1) - diff(f)
                fluxes[f] = flux(row(f - 1), diff(f), curvature, sine * sy[f])
            return fluxes[f]

        for r in row_list:
            y_buf[direction, r] = row(r) - (face(r + 1) - face(r))

    def sweep_y_all(step, row_list):
        def body(positive):
            def one(direction, carry):
                sweep_y(step, direction, positive, row_list)
                return carry

            return one

        lax.fori_loop(0, SIN_POS, body(True), 0)
        lax.fori_loop(SIN_POS, ND, body(False), 0)

    inner = tuple(range(2, 6))
    outer = (0, 1, 6, 7)

    def receive_tile(kind):
        def body(tile, carry):
            turn_points(tile, kind == 0)
            for s in range(FOLD):
                place(FOLD * tile + s, tile, s)
            for copy in tile_halos(tile, kind):
                copy.start()
            for s in range(FOLD):
                positive = kind == 0 or (kind == 1 and FOLD * tile + s < SIN_POS)
                sweep_y(0, FOLD * tile + s, positive, inner)
            return carry

        return body

    middle = SIN_POS // FOLD
    assert middle == EARLY
    lax.fori_loop(0, middle, receive_tile(0), 0)
    place(LAST, None, None)
    for copy in tile_halos(TILES, 2):
        copy.start()
    sweep_y(0, LAST, False, inner)
    receive_tile(1)(middle, 0)
    lax.fori_loop(middle + 1, TILES, receive_tile(2), 0)

    def sweep_theta(step, r):
        t = trn[pl.ds(pl.multiple_of(8 * r, 8), 8), :]
        forward = t >= 0.0
        q = [y_buf[j, r] for j in range(ND)]
        d = [q[(j + 1) % ND] - q[j] for j in range(ND)]

        def face(j):
            ahead = d[(j + 1) % ND] - d[j]
            behind = d[j] - d[j - 1]
            if TURN[j] >= 0:
                curvature = jnp.where(forward, behind, ahead)
            else:
                curvature = jnp.where(forward, ahead, behind)
            return flux(q[j], d[j], curvature, float(TURN[j]) * t)

        last = face(ND - 1)
        prior = last
        for j in range(ND):
            f = last if j == ND - 1 else face(j)
            value = q[j] - (f - prior)
            prior = f
            if step == 0:
                sign = 1 if COS[j] >= 0 else -1
                x_ext[1, j, r + 2] = sweep_x(value, float(COS[j]) * sx[r], sign, sub, lane)
            else:
                y_buf[j, r] = value

    def theta_inner(step):
        def body(r, carry):
            sweep_theta(step, r)
            return carry

        lax.fori_loop(2, 6, body, 0)

    def theta_outer(step):
        def body(k, carry):
            sweep_theta(step, k + 4 * (k // 2))
            return carry

        lax.fori_loop(0, 4, body, 0)

    theta_inner(0)
    for tile in range(TILES + 1):
        for copy in tile_halos(tile, 0 if tile < middle else 1 if tile == middle else 2):
            copy.wait()
    sweep_y_all(0, outer)
    theta_outer(0)
    for copy in second_halos():
        copy.start()
    sweep_y_all(1, inner)
    theta_inner(1)
    for copy in second_halos():
        copy.wait()
    sweep_y_all(1, outer)
    theta_outer(1)

    def collect(direction, tile, s):
        taken = [lanes(y_buf[direction, v], take_at[v]) for v in range(ROWS)]
        for u in range(3):
            for h in range(2):
                index = back_row[u, h]
                which = back_tile[u, h]
                value = None
                for v in ROW_TILES[u]:
                    got = sublanes(taken[v], index)
                    value = got if value is None else jnp.where(which == v, got, value)
                if s is None:
                    p_buf[u, h, 120:128, :] = value
                else:
                    p_buf[tile, h, BUCKET * s + 8 * u : BUCKET * s + 8 * u + 8, :] = value

    def third_ends(tile, peer, early):
        source_ref = z_buf.at[tile, peer] if early else r_buf.at[tile, peer]
        return source_ref, n_buf.at[tile, me_l]

    def third_copy(tile, r, early):
        peer = (me_l + r) % NL
        source_ref, target_ref = third_ends(tile, peer, early)
        return pltpu.make_async_remote_copy(
            src_ref=source_ref,
            dst_ref=target_ref,
            send_sem=third_send.at[tile],
            recv_sem=third_recv.at[tile],
            device_id={"comp": me_c, "lat": peer},
            device_id_type=pl.DeviceIdType.MESH,
        )

    def third_local(tile, early):
        source_ref, target_ref = third_ends(tile, me_l, early)
        return pltpu.make_async_copy(source_ref, target_ref, third_own.at[tile])

    def third_send_all(tile, early):
        for r in range(1, NL):
            third_copy(tile, r, early).start()
        third_local(tile, early).start()

    def back_ends(tile, peer):
        return r_buf.at[tile, :, slot_of(peer), :], z_buf.at[tile, :, me_c, :]

    def back_copy(tile, r):
        peer = (me_c + r) % NC
        source_ref, target_ref = back_ends(tile, peer)
        return pltpu.make_async_remote_copy(
            src_ref=source_ref,
            dst_ref=target_ref,
            send_sem=back_send.at[tile],
            recv_sem=back_recv.at[tile],
            device_id={"comp": peer, "lat": me_l},
            device_id_type=pl.DeviceIdType.MESH,
        )

    def back_local(tile):
        source_ref, target_ref = back_ends(tile, me_c)
        return pltpu.make_async_copy(source_ref, target_ref, back_own.at[tile])

    def collect_tile(early):
        def body(tile, carry):
            for s in range(FOLD):
                collect(FOLD * tile + s, tile, s)
            for h in range(2):
                r_rows[tile, pl.ds(h, 128, stride=2), :] = p_buf[tile, h].T
            if early:
                for r in range(1, NC):
                    back_copy(tile, r).start()
                back_local(tile).start()
            else:
                third_send_all(tile, False)
            return carry

        return body

    def back_tile_on(tile, carry):
        cross_many(z_buf, tile, back_recv).wait()
        back_local(tile).wait()
        third_send_all(tile, True)
        return carry

    lax.fori_loop(EARLY, EARLY + 1, collect_tile(False), 0)
    collect(LAST, None, None)
    lax.fori_loop(0, EARLY, collect_tile(True), 0)
    lax.fori_loop(EARLY + 1, TILES, collect_tile(False), 0)
    lax.fori_loop(0, EARLY, back_tile_on, 0)

    def put(direction, parts, early):
        for u in range(6):
            at = own_put_at[u] if early else put_at[u]
            which = own_put_tile[u] if early else put_tile[u]
            value = jnp.zeros((8, 128), jnp.float32)
            for v in range(TILES):
                if u in SLOT_TILES[v]:
                    value = jnp.where(which == v, lanes(parts[v], at), value)
            columns = pl.ds(128 * u, 128)
            if early:
                out[direction, :, columns] = value
            else:
                o_buf[direction, :, columns] = value

    def fourth_ends(k, peer):
        part = chunk(k)
        return o_buf.at[part, slot_of(peer), :], out.at[part, me_c, :]

    def fourth_copy(k, r):
        peer = (me_c + r) % NC
        source_ref, target_ref = fourth_ends(k, peer)
        return pltpu.make_async_remote_copy(
            src_ref=source_ref,
            dst_ref=target_ref,
            send_sem=fourth_send.at[k],
            recv_sem=fourth_recv.at[k],
            device_id={"comp": peer, "lat": me_l},
            device_id_type=pl.DeviceIdType.MESH,
        )

    def fourth_local(k):
        source_ref, target_ref = fourth_ends(k, me_c)
        return pltpu.make_async_copy(source_ref, target_ref, fourth_own.at[k])

    def fourth_send_all(k):
        for r in range(1, NC):
            fourth_copy(k, r).start()
        fourth_local(k).start()

    def put_tile_of(early):
        def body(tile, carry):
            many(n_buf, tile, third_recv).wait()
            third_local(tile, early).wait()
            swapped = []
            for v in range(TILES):
                parts = [n_buf[tile, min(FOLD * v + b, NL - 1)] for b in range(FOLD)]
                swapped.append(swap_blocks(parts, block_masks, turns))
            for s in range(FOLD):
                put(FOLD * tile + s, [swapped[v][s] for v in range(TILES)], early)
            if not early:
                fourth_send_all(tile)
            return carry

        return body

    def put_last():
        parts = []
        spare = 120 + (lane & 7)
        for v in range(TILES):
            value = jnp.zeros((8, 128), jnp.float32)
            for b in range(FOLD):
                if FOLD * v + b < NL:
                    for e in range(3):
                        got = lanes(n_buf[e, FOLD * v + b], spare)
                        value = jnp.where((lane >> 3) == 3 * b + e, got, value)
            parts.append(value)
        put(LAST, parts, True)

    lax.fori_loop(EARLY, TILES, put_tile_of(False), 0)
    lax.fori_loop(0, EARLY, put_tile_of(True), 0)
    put_last()

    for g in range(EARLY, TILES):
        first_wait(g, first_send).wait()
    for tile in range(TILES):
        many(r_buf, tile, second_send).wait()
        many(n_buf, tile, third_send).wait()
    for tile in range(EARLY):
        cross_many(r_buf, tile, cross_send).wait()
        cross_many(z_buf, tile, back_send).wait()
    for k in range(EARLY, TILES):
        fourth_local(k).wait()
        part = out.at[chunk(k), pl.ds(0, NC - 1), :]
        pltpu.make_async_copy(part, part, fourth_recv.at[k]).wait()
        pltpu.make_async_copy(part, part, fourth_send.at[k]).wait()


def per_device(spectra_in, group_speed, turn_rate, sea_mask, sea_cell, slab_counts):
    f32 = jnp.float32
    vreg = (8, 128)
    dma = pltpu.SemaphoreType.DMA
    hbm = pl.BlockSpec(memory_space=pltpu.HBM)
    return pl.pallas_call(
        kernel,
        out_shape=pltpu.VMEM((ND, NC, SLOTS), f32),
        in_specs=[hbm] * 6,
        out_specs=pl.BlockSpec(memory_space=pltpu.VMEM),
        scratch_shapes=[
            pltpu.VMEM((1, ROWS, 1024), f32),
            pltpu.VMEM((1, ROWS, 1024), f32),
            pltpu.VMEM((ROWS, 1024), jnp.int32),
            pltpu.VMEM((48, 128), jnp.int32),
            pltpu.SMEM((NL,), jnp.int32),
            pltpu.SMEM((2, ND), f32),
            dma((7,)),
            pltpu.VMEM((ND, NC, SLOTS), f32),
            pltpu.VMEM((ND, NC, SLOTS), f32),
            pltpu.VMEM((NL, TILES) + vreg, f32),
            pltpu.VMEM((EARLY, NL) + vreg, f32),
            pltpu.VMEM((TILES, NL) + vreg, f32),
            pltpu.VMEM((TILES, 2, 128, 128), f32),
            pltpu.VMEM((EARLY, NL) + vreg, f32),
            pltpu.VMEM((TILES, NL) + vreg, f32),
            pltpu.VMEM((ND, NC, SLOTS), f32),
            pltpu.VMEM((2, ND, ROWS + 4) + vreg, f32),
            pltpu.VMEM((ND, ROWS) + vreg, f32),
            pltpu.VMEM((64, 128), f32),
            pltpu.VMEM((64, 128), f32),
            pltpu.VMEM((64, 128), f32),
            pltpu.VMEM((4,) + vreg, f32),
            pltpu.VMEM((ROWS,) + vreg, f32),
            pltpu.VMEM((ROWS + 1,) + vreg, f32),
            pltpu.VMEM((TILES,) + vreg, jnp.int32),
            pltpu.VMEM((TILES,) + vreg, jnp.int32),
            pltpu.VMEM((6,) + vreg, jnp.int32),
            pltpu.VMEM((6,) + vreg, jnp.int32),
            pltpu.VMEM((6,) + vreg, jnp.int32),
            pltpu.VMEM((6,) + vreg, jnp.int32),
            pltpu.VMEM((ROWS,) + vreg, jnp.int32),
            pltpu.VMEM((ROWS,) + vreg, jnp.int32),
            pltpu.VMEM((ROWS,) + vreg, jnp.int32),
            pltpu.VMEM((ROWS,) + vreg, jnp.int32),
            pltpu.VMEM((3, 2) + vreg, jnp.int32),
            pltpu.VMEM((3, 2) + vreg, jnp.int32),
            pltpu.VMEM((TILES,) + vreg, f32),
            dma((TILES,)), dma((TILES,)), dma((TILES,)),
            dma((TILES,)), dma((TILES,)), dma((TILES,)),
            dma((EARLY,)), dma((EARLY,)), dma((EARLY,)),
            dma((EARLY,)), dma((EARLY,)), dma((EARLY,)),
            dma((4,)), dma((4,)), dma((2, 2 * TILES + 2)), dma((2, 2 * TILES + 2)),
            dma((TILES,)), dma((TILES,)), dma((TILES,)),
            dma((TILES,)), dma((TILES,)), dma((TILES,)),
        ],
        compiler_params=pltpu.CompilerParams(
            collective_id=0, has_side_effects=True, vmem_limit_bytes=64000 * 1024
        ),
        name="wave_step",
    )(
        spectra_in.transpose(1, 0, 2),
        group_speed,
        turn_rate,
        sea_mask,
        sea_cell.reshape(48, 128),
        slab_counts,
    ).transpose(1, 0, 2)


def solution(mesh):
    in_specs = (
        P(None, None, ("comp", "lat")),
        P("comp", "lat", None),
        P("comp", "lat", None),
        P("lat", None),
        P("lat"),
        P(),
    )
    out_specs = P(None, None, ("comp", "lat"))
    return jax.shard_map(
        per_device, mesh=mesh, in_specs=in_specs, out_specs=out_specs, check_vma=False
    )
```

```python
import math

import jax
import jax.numpy as jnp
import numpy as np
from jax import lax
from jax.experimental import pallas as pl
from jax.experimental.pallas import tpu as pltpu
from jax.sharding import PartitionSpec as P

NC = 8
NL = 32
ND = 36
SLOTS = 768
BUCKET = 24
ROWS = 8
FOLD = 5
TILES = 7
EARLY = 3
LAST = ND - 1
PARTS = ((0, 12), (12, 12), (24, 12))
BEFORE = ((34, 16), (14, 12), (26, 8))
SIN_POS = 19

ANGLES = np.arange(ND, dtype=np.float32) * np.float32(2.0 * math.pi / ND)
COS = np.cos(ANGLES).astype(np.float32)
SIN = np.sin(ANGLES).astype(np.float32)
TURN = (0.5 * (COS + np.roll(COS, -1))).astype(np.float32)
assert (SIN[:SIN_POS] >= 0).all() and (SIN[SIN_POS:] < 0).all()

SLOT_TILES = ((0,), (0, 1), (0, 1, 2), (1, 2, 3), (1, 2, 3, 4), (2, 3, 4, 5), (2, 3, 4, 5))
POINT_TILES = tuple(
    tuple(range(max(0, 4 * v - 20) // 8, min(2, (4 * v + 3) // 8) + 1)) for v in range(ROWS)
)
ROW_TILES = tuple(tuple(range(2 * u, min(7, 2 * u + 6) + 1)) for u in range(3))


def ranges(first, number):
    cuts = []
    for j in range(first, first + number):
        j = j % ND
        if cuts and j == cuts[-1][0] + cuts[-1][1] and j not in (0, SIN_POS):
            cuts[-1][1] += 1
        else:
            cuts.append([j, 1])
    return [(low, size, low < SIN_POS) for low, size in cuts]


SECOND_HALOS = [ranges(*p) for p in PARTS]
HALOS = 2 * (TILES + 1)
assert sum(len(r) for r in SECOND_HALOS) <= TILES + 1


def lanes(values, index):
    return jnp.take_along_axis(values, index, axis=1)


def sublanes(values, index):
    return jnp.take_along_axis(values, index, axis=0)


def iotas():
    return (
        lax.broadcasted_iota(jnp.int32, (8, 128), 0),
        lax.broadcasted_iota(jnp.int32, (8, 128), 1),
    )


def swap_blocks(parts, block_masks, turns):
    rolled = []
    for k in range(FOLD):
        diagonal = parts[(FOLD - 1 + k) % FOLD]
        for b in range(FOLD - 1):
            diagonal = jnp.where(block_masks[b], parts[(b + k) % FOLD], diagonal)
        rolled.append(diagonal if k == 0 else lanes(diagonal, turns[k]))
    outs = []
    for a in range(FOLD):
        value = rolled[(FOLD - 1 - a) % FOLD]
        for b in range(FOLD - 1):
            value = jnp.where(block_masks[b], rolled[(b - a) % FOLD], value)
        outs.append(value)
    return outs


def flux(q, d, curvature, c):
    sixth = 1.0 / 6.0
    return c * (q + (1.0 - c) * (0.5 * d - (c * sixth + sixth) * curvature))


def sweep_x(q, c, sign, sub, lane):
    east = lanes(q, (lane + 1) & 127)
    east = jnp.where(lane == 127, sublanes(east, (sub + 1) & 7), east)
    east = jnp.where((lane == 127) & (sub == 7), 0.0, east)
    d = east - q
    side = lanes(d, (lane - sign) & 127)
    edge = lane == jnp.where(sign > 0, 0, 127)
    side = jnp.where(edge, sublanes(side, (sub - sign) & 7), side)
    side = jnp.where(edge & (sub == jnp.where(sign > 0, 0, 7)), q, side)
    curvature = (d - side) * jnp.where(sign > 0, 1.0, -1.0)
    f = flux(q, d, curvature, c)
    west = lanes(f, (lane - 1) & 127)
    west = jnp.where(lane == 0, sublanes(west, (sub - 1) & 7), west)
    return q - (f - west)


def kernel(
    spectra, speed_in, turn_in, mask_in, cells_in, counts_in, out,
    speed, turn, mask, cells, counts, trig, load_sem,
    a_buf, own_buf, m_buf, x_buf, r_buf, p_buf, z_buf, n_buf, o_buf, x_ext, y_buf, done,
    spd, trn, msk, stat_halo, sx, sy,
    pack_at, own_at, put_at, put_tile, own_put_at, own_put_tile, row_at, row_tile, lane_at, take_at, back_row, back_tile, w_last,
    first_send, first_recv, first_own, second_send, second_recv, second_own,
    cross_send, cross_recv, cross_own, back_send, back_recv, back_own,
    stat_send, stat_recv, halo_send, halo_recv,
    third_send, third_recv, third_own, fourth_send, fourth_recv, fourth_own,
):
    me_c = lax.axis_index("comp")
    me_l = lax.axis_index("lat")
    sub, lane = iotas()

    def slot_of(c):
        return (c % 4) * 2 + c // 4

    loads = [
        pltpu.make_async_copy(source_ref, target_ref, load_sem.at[k])
        for k, (source_ref, target_ref) in enumerate(
            (
                (counts_in, counts),
                (spectra.at[pl.ds(0, FOLD * EARLY)], own_buf.at[pl.ds(0, FOLD * EARLY)]),
                (spectra.at[pl.ds(LAST, 1)], own_buf.at[pl.ds(LAST, 1)]),
                (speed_in, speed),
                (turn_in, turn),
                (mask_in, mask),
                (cells_in, cells),
            )
        )
    ]
    for load in loads:
        load.start()

    def chunk(tile):
        return pl.ds(FOLD * tile, FOLD)

    def first_ends(g, peer):
        return spectra.at[chunk(g), peer, :], a_buf.at[chunk(g), slot_of(me_c), :]

    def first_local(g):
        source_ref, target_ref = first_ends(g, me_c)
        return pltpu.make_async_copy(source_ref, target_ref, first_own.at[g])

    for g in range(EARLY, TILES):
        first_local(g).start()

    barrier = pltpu.get_barrier_semaphore()

    def greet_comp(r, carry):
        pl.semaphore_signal(
            barrier, inc=1, device_id={"comp": (me_c + r) % NC, "lat": me_l}, device_id_type=pl.DeviceIdType.MESH
        )
        return carry

    def greet_lat(r, carry):
        pl.semaphore_signal(
            barrier, inc=1, device_id={"comp": me_c, "lat": (me_l + r) % NL}, device_id_type=pl.DeviceIdType.MESH
        )
        return carry

    lax.fori_loop(1, NC, greet_comp, 0)
    lax.fori_loop(1, NL, greet_lat, 0)

    for j in range(ND):
        trig[0, j] = jnp.float32(float(COS[j]))
        trig[1, j] = jnp.float32(float(SIN[j]))

    for load in loads:
        load.wait()
    starts = [jnp.int32(0)]
    for slab in range(NL):
        starts.append(starts[-1] + counts[slab])
    own_start = jnp.int32(0)
    for slab in range(NL):
        own_start = own_start + jnp.where(slab < me_l, counts[slab], 0)

    source = ((sub & 1) * 4 + (sub >> 1)) * NL + me_l
    own_source = me_c * NL + me_l
    block = (lane * 171) >> 12
    in_block = lane - block * BUCKET
    block_masks = [block == b for b in range(FOLD)]
    turns = [None] + [
        jnp.where(lane >= BUCKET * k, lane - BUCKET * k, lane - BUCKET * k + BUCKET * FOLD) & 127
        for k in range(1, FOLD)
    ]
    for v in range(TILES):
        base = jnp.full((8, 128), starts[min(FOLD * v, NL - 1)], jnp.int32)
        for b in range(1, FOLD):
            if FOLD * v + b < NL:
                base = jnp.where(block == b, starts[FOLD * v + b], base)
        pack_at[v] = ((base - source + 255) >> 8) + in_block
        own_at[v] = ((base - own_source + 255) >> 8) + in_block

    for t in range(8):
        columns = pl.ds(128 * t, 128)
        spd[pl.ds(t, 8, stride=8), :] = speed[0, :, columns]
        trn[pl.ds(t, 8, stride=8), :] = turn[0, :, columns]
        msk[pl.ds(t, 8, stride=8), :] = mask[:, columns].astype(jnp.float32)

    for u in range(6):
        for origin, at, which in ((source, put_at, put_tile), (own_source, own_put_at, own_put_tile)):
            point = origin + (lane + 128 * u) * 256
            slab = jnp.zeros((8, 128), jnp.int32)
            begin = jnp.zeros((8, 128), jnp.int32)
            for s in range(1, NL + 1):
                past = point >= starts[s]
                slab = jnp.where(past, s, slab)
                begin = jnp.where(past, starts[s], begin)
            nth = lane + 128 * u - ((begin - origin + 255) >> 8)
            tile = (slab * 205) >> 10
            at[u] = ((slab - tile * FOLD) * BUCKET + nth) & 127
            which[u] = jnp.where(slab < NL, tile, -1)

    ones = jnp.ones((128, 128), jnp.bfloat16)
    deep = lax.broadcasted_iota(jnp.int32, (128, 128), 0)
    wide = lax.broadcasted_iota(jnp.int32, (128, 128), 1)
    before = jnp.where(deep < wide, 1.0, 0.0).astype(jnp.bfloat16)
    above = jnp.where(wide < deep, 1.0, 0.0).astype(jnp.bfloat16)[:64, :64]
    sea = msk[...].astype(jnp.bfloat16)
    inside = jnp.dot(sea, before, preferred_element_type=jnp.float32)
    totals = jnp.dot(sea, ones, preferred_element_type=jnp.float32)
    offsets = jnp.dot(above, totals.astype(jnp.bfloat16), preferred_element_type=jnp.float32)
    inside = inside.astype(jnp.int32)
    offsets = offsets.astype(jnp.int32)
    low_source = (lane & 3) * NL + (lane >> 2)
    for v in range(ROWS):
        offset = offsets[8 * v : 8 * v + 8]
        point = offset + inside[8 * v : 8 * v + 8] + own_start
        lane_at[v] = ((point & 31) << 2) | ((point >> 5) & 3)
        point = offset + ((low_source - own_start - offset) & 127)
        row_at[v] = (point >> 8) & 7
        row_tile[v] = ((point >> 11) << 1) + (((point + own_start) >> 7) & 1)
    cell_at = []
    for u in range(3):
        even = cells[pl.ds(16 * u, 8, stride=2), :]
        odd = cells[pl.ds(16 * u + 1, 8, stride=2), :]
        for h in range(2):
            rho = (low_source + 128 * h - own_start) & 255
            cell = jnp.where(rho < 128, lanes(even, rho & 127), lanes(odd, rho & 127))
            cell_at.append(cell)
            back_row[u, h] = (cell >> 7) & 7
            back_tile[u, h] = cell >> 10
    for v in range(ROWS):
        index = row_at[v]
        which = row_tile[v]
        value = jnp.zeros((8, 128), jnp.int32)
        for u in POINT_TILES[v]:
            for h in range(2):
                value = jnp.where(which == 2 * u + h, sublanes(cell_at[2 * u + h], index), value)
        take_at[v] = value & 127

    for v in range(ROWS):
        rows = pl.ds(8 * v, 8)
        s = spd[rows, :]
        m = msk[rows, :]

        def eastward(x):
            east = lanes(x, (lane + 1) & 127)
            return jnp.where(lane == 127, sublanes(east, (sub + 1) & 7), east)

        face = 0.5 * (s + eastward(s)) * m * eastward(m)
        sx[v] = jnp.where((lane == 127) & (sub == 7), 0.0, face)
        trn[rows, :] = trn[rows, :] * m
        if v < ROWS - 1:
            after = pl.ds(8 * v + 8, 8)
            sy[v + 1] = 0.5 * (s + spd[after, :]) * m * msk[after, :]
    def slot_rows(buffer, direction):
        return [buffer[direction, :, pl.ds(128 * u, 128)] for u in range(6)]

    def windows(at_ref, v, rows):
        at = at_ref[v]
        low = at & 127
        value = None
        for u in SLOT_TILES[v]:
            got = lanes(rows[u], low)
            value = got if value is None else jnp.where((at >> 7) == u, got, value)
        return value

    def pack(tile, early):
        buffer, at_ref = (own_buf, own_at) if early else (a_buf, pack_at)
        rows = [slot_rows(buffer, FOLD * tile + s) for s in range(FOLD)]
        for v in range(TILES):
            parts = [windows(at_ref, v, rows[s]) for s in range(FOLD)]
            for b, value in enumerate(swap_blocks(parts, block_masks, turns)):
                if FOLD * v + b < NL:
                    if early:
                        extra = lanes(w_last[v], BUCKET * b + 8 * tile + (lane & 7))
                        value = jnp.where(lane >= 120, extra, value)
                    m_buf[FOLD * v + b, tile] = value

    def pack_early(tile, carry):
        pack(tile, True)
        return carry

    last_rows = slot_rows(own_buf, LAST)
    for v in range(TILES):
        w_last[v] = windows(own_at, v, last_rows)
    lax.fori_loop(0, EARLY, pack_early, 0)

    pl.semaphore_wait(barrier, NC - 1 + NL - 1)

    def first_wait(g, sem):
        ref = a_buf.at[chunk(g), pl.ds(0, NC - 1), :]
        return pltpu.make_async_copy(ref, ref, sem.at[g])

    def first_copy(g, r):
        peer = (me_c + r) % NC
        source_ref, target_ref = first_ends(g, peer)
        return pltpu.make_async_remote_copy(
            src_ref=source_ref,
            dst_ref=target_ref,
            send_sem=first_send.at[g],
            recv_sem=first_recv.at[g],
            device_id={"comp": peer, "lat": me_l},
            device_id_type=pl.DeviceIdType.MESH,
        )


    north = {"comp": me_c, "lat": (me_l + 1) % NL}
    south = {"comp": me_c, "lat": (me_l + NL - 1) % NL}

    def stat_copy(k):
        ref = (spd, msk)[k % 2]
        row = 56 if k < 2 else 0
        return pltpu.make_async_remote_copy(
            src_ref=ref.at[pl.ds(row, 8), :],
            dst_ref=stat_halo.at[k],
            send_sem=stat_send.at[k],
            recv_sem=stat_recv.at[k],
            device_id=north if k < 2 else south,
            device_id_type=pl.DeviceIdType.MESH,
        )


    def second_copy(tile, r, early):
        peer = (me_l + r) % NL
        return pltpu.make_async_remote_copy(
            src_ref=m_buf.at[peer, tile],
            dst_ref=x_buf.at[tile, me_l] if early else r_buf.at[tile, me_l],
            send_sem=second_send.at[tile],
            recv_sem=second_recv.at[tile],
            device_id={"comp": me_c, "lat": peer},
            device_id_type=pl.DeviceIdType.MESH,
        )

    def second_local(tile, early):
        return pltpu.make_async_copy(
            m_buf.at[me_l, tile],
            x_buf.at[tile, me_l] if early else r_buf.at[tile, me_l],
            second_own.at[tile],
        )

    def many(ref, tile, sem):
        part = ref.at[tile, pl.ds(0, NL - 1)]
        return pltpu.make_async_copy(part, part, sem.at[tile])

    def send_tile(early):
        def body(tile, carry):
            if not early:
                first_wait(tile, first_recv).wait()
                first_local(tile).wait()
                pack(tile, False)
            for r in range(1, NL):
                second_copy(tile, r, early).start()
            second_local(tile, early).start()
            return carry

        return body

    for g in range(EARLY, TILES):
        for r in range(1, NC):
            first_copy(g, r).start()
    for k in range(4):
        stat_copy(k).start()
    lax.fori_loop(0, EARLY, send_tile(True), 0)
    lax.fori_loop(EARLY, TILES, send_tile(False), 0)

    def cross_ends(tile, peer):
        return x_buf.at[tile, :, peer, :], r_buf.at[tile, :, slot_of(me_c), :]

    def cross_copy(tile, r):
        peer = (me_c + r) % NC
        source_ref, target_ref = cross_ends(tile, peer)
        return pltpu.make_async_remote_copy(
            src_ref=source_ref,
            dst_ref=target_ref,
            send_sem=cross_send.at[tile],
            recv_sem=cross_recv.at[tile],
            device_id={"comp": peer, "lat": me_l},
            device_id_type=pl.DeviceIdType.MESH,
        )

    def cross_local(tile):
        source_ref, target_ref = cross_ends(tile, me_c)
        return pltpu.make_async_copy(source_ref, target_ref, cross_own.at[tile])

    def cross_many(ref, tile, sem):
        part = ref.at[tile, :, pl.ds(0, NC - 1), :]
        return pltpu.make_async_copy(part, part, sem.at[tile])

    def cross_tile(tile, carry):
        many(x_buf, tile, second_recv).wait()
        second_local(tile, True).wait()
        for r in range(1, NC):
            cross_copy(tile, r).start()
        cross_local(tile).start()
        return carry

    lax.fori_loop(0, EARLY, cross_tile, 0)

    for k in range(4):
        stat_copy(k).wait()
    south_mask = jnp.where(me_l > 0, stat_halo[1], 0.0)
    north_mask = jnp.where(me_l < NL - 1, stat_halo[3], 0.0)
    sy[0] = 0.5 * (stat_halo[0] + spd[0:8, :]) * south_mask * msk[0:8, :]
    sy[8] = 0.5 * (stat_halo[2] + spd[56:64, :]) * north_mask * msk[56:64, :]

    r_rows = r_buf.reshape(TILES, NL * 8, 128)

    def turn_points(tile, early):
        if early:
            cross_many(r_buf, tile, cross_recv).wait()
            cross_local(tile).wait()
        else:
            many(r_buf, tile, second_recv).wait()
            second_local(tile, False).wait()
        for h in range(2):
            p_buf[tile, h] = r_rows[tile, pl.ds(h, 128, stride=2), :].T

    def point_ref(tile, s, u, h):
        if s is None:
            return p_buf.at[tile[u], h, pl.ds(120, 8), :]
        return p_buf.at[tile, h, pl.ds(pl.multiple_of(BUCKET * s + 8 * u, 8), 8), :]

    def place(direction, tile, s):
        held = {(u, h): point_ref(tile, s, u, h)[...] for u in range(3) for h in range(2)}
        cosine = trig[0, direction]
        sign = jnp.where(cosine >= 0.0, 1, -1)
        for v in range(ROWS):
            index = row_at[v]
            which = row_tile[v]
            value = None
            for u in POINT_TILES[v]:
                for h in range(2):
                    got = sublanes(held[u, h], index)
                    value = got if value is None else jnp.where(which == 2 * u + h, got, value)
            q = jnp.where(msk[pl.ds(8 * v, 8), :] > 0.0, lanes(value, lane_at[v]), 0.0)
            x_ext[0, direction, v + 2] = sweep_x(q, cosine * sx[v], sign, sub, lane)

    def halo_copy(step, dirs, rows, to_north, k):
        source_row = 2 + ROWS - rows if to_north else 2
        target_row = 2 - rows if to_north else 2 + ROWS
        return pltpu.make_async_remote_copy(
            src_ref=x_ext.at[step, dirs, pl.ds(source_row, rows)],
            dst_ref=x_ext.at[step, dirs, pl.ds(target_row, rows)],
            send_sem=halo_send.at[step, k],
            recv_sem=halo_recv.at[step, k],
            device_id=north if to_north else south,
            device_id_type=pl.DeviceIdType.MESH,
        )

    def tile_halos(tile, kind):
        north_rows, south_rows = ((2, 1), (2, 2), (1, 2))[kind]
        dirs = pl.ds(FOLD * tile, 1 if isinstance(tile, int) and tile == TILES else FOLD)
        return (
            halo_copy(0, dirs, north_rows, True, 2 * tile),
            halo_copy(0, dirs, south_rows, False, 2 * tile + 1),
        )

    def second_halos(part):
        k = 2 * sum(len(r) for r in SECOND_HALOS[:part])
        copies = []
        for low, size, positive in SECOND_HALOS[part]:
            dirs = pl.ds(low, size)
            copies.append(halo_copy(1, dirs, 2 if positive else 1, True, k))
            copies.append(halo_copy(1, dirs, 1 if positive else 2, False, k + 1))
            k += 2
        return copies

    def sweep_y(step, direction, positive, row_list):
        sine = trig[1, direction]

        def row(r):
            value = x_ext[step, direction, r + 2]
            if r < 0:
                value = jnp.where(me_l > 0, value, 0.0)
            if r >= ROWS:
                value = jnp.where(me_l < NL - 1, value, 0.0)
            return value

        diffs = {}
        fluxes = {}

        def diff(f):
            if f not in diffs:
                diffs[f] = row(f) - row(f - 1)
            return diffs[f]

        def face(f):
            if f not in fluxes:
                if positive:
                    curvature = diff(f) - diff(f - 1)
                else:
                    curvature = diff(f + 1) - diff(f)
                fluxes[f] = flux(row(f - 1), diff(f), curvature, sine * sy[f])
            return fluxes[f]

        for r in row_list:
            y_buf[direction, r] = row(r) - (face(r + 1) - face(r))

    def sweep_y_of(step, cuts, row_list):
        for low, size, positive in cuts:

            def body(direction, carry, positive=positive):
                sweep_y(step, direction, positive, row_list)
                return carry

            lax.fori_loop(low, low + size, body, 0)

    def sweep_theta(step, first, number, r):
        t = trn[pl.ds(pl.multiple_of(8 * r, 8), 8), :]
        forward = t >= 0.0
        q = {k: y_buf[k % ND, r] for k in range(first - 2, first + number + 2)}
        d = {k: q[k + 1] - q[k] for k in range(first - 2, first + number + 1)}

        def face(k):
            ahead = d[k + 1] - d[k]
            behind = d[k] - d[k - 1]
            turning = float(TURN[k % ND])
            if turning >= 0:
                curvature = jnp.where(forward, behind, ahead)
            else:
                curvature = jnp.where(forward, ahead, behind)
            return flux(q[k], d[k], curvature, turning * t)

        prior = face(first - 1)
        for k in range(first, first + number):
            f = face(k)
            value = q[k] - (f - prior)
            prior = f
            j = k % ND
            if step == 0:
                sign = 1 if COS[j] >= 0 else -1
                x_ext[1, j, r + 2] = sweep_x(value, float(COS[j]) * sx[r], sign, sub, lane)
            else:
                done[j, r] = value

    inner = tuple(range(2, 6))
    outer = (0, 1, 6, 7)

    def theta_inner(step):
        def body(r, carry):
            sweep_theta(step, 0, ND, r)
            return carry

        lax.fori_loop(2, 6, body, 0)

    def theta_outer(step, first, number):
        def body(k, carry):
            sweep_theta(step, first, number, k)
            sweep_theta(step, first, number, k + 6)
            return carry

        lax.fori_loop(0, 2, body, 0)

    def receive_tile(kind):
        def body(tile, carry):
            turn_points(tile, kind == 0)
            for s in range(FOLD):
                place(FOLD * tile + s, tile, s)
            for copy in tile_halos(tile, kind):
                copy.start()
            for s in range(FOLD):
                positive = kind == 0 or (kind == 1 and FOLD * tile + s < SIN_POS)
                sweep_y(0, FOLD * tile + s, positive, inner)
            return carry

        return body

    middle = SIN_POS // FOLD
    assert middle == EARLY
    lax.fori_loop(0, middle, receive_tile(0), 0)
    place(LAST, range(EARLY), None)
    for copy in tile_halos(TILES, 2):
        copy.start()
    sweep_y(0, LAST, False, inner)
    receive_tile(1)(middle, 0)
    lax.fori_loop(middle + 1, TILES, receive_tile(2), 0)

    theta_inner(0)
    for tile in range(TILES + 1):
        for copy in tile_halos(tile, 0 if tile < middle else 1 if tile == middle else 2):
            copy.wait()
    for part in range(len(PARTS)):
        sweep_y_of(0, ranges(*BEFORE[part]), outer)
        theta_outer(0, *PARTS[part])
        for copy in second_halos(part):
            copy.start()
    sweep_y_of(1, ranges(0, ND), inner)
    theta_inner(1)

    def collect(direction, tile, s):
        taken = [lanes(done[direction, v], take_at[v]) for v in range(ROWS)]
        for u in range(3):
            for h in range(2):
                index = back_row[u, h]
                which = back_tile[u, h]
                value = None
                for v in ROW_TILES[u]:
                    got = sublanes(taken[v], index)
                    value = got if value is None else jnp.where(which == v, got, value)
                point_ref(tile, s, u, h)[...] = value

    def third_ends(tile, peer, early):
        source_ref = z_buf.at[tile, peer] if early else r_buf.at[tile, peer]
        return source_ref, n_buf.at[tile, me_l]

    def third_copy(tile, r, early):
        peer = (me_l + r) % NL
        source_ref, target_ref = third_ends(tile, peer, early)
        return pltpu.make_async_remote_copy(
            src_ref=source_ref,
            dst_ref=target_ref,
            send_sem=third_send.at[tile],
            recv_sem=third_recv.at[tile],
            device_id={"comp": me_c, "lat": peer},
            device_id_type=pl.DeviceIdType.MESH,
        )

    def third_local(tile, early):
        source_ref, target_ref = third_ends(tile, me_l, early)
        return pltpu.make_async_copy(source_ref, target_ref, third_own.at[tile])

    def third_send_all(tile, early):
        for r in range(1, NL):
            third_copy(tile, r, early).start()
        third_local(tile, early).start()

    def back_ends(tile, peer):
        return r_buf.at[tile, :, slot_of(peer), :], z_buf.at[tile, :, me_c, :]

    def back_copy(tile, r):
        peer = (me_c + r) % NC
        source_ref, target_ref = back_ends(tile, peer)
        return pltpu.make_async_remote_copy(
            src_ref=source_ref,
            dst_ref=target_ref,
            send_sem=back_send.at[tile],
            recv_sem=back_recv.at[tile],
            device_id={"comp": peer, "lat": me_l},
            device_id_type=pl.DeviceIdType.MESH,
        )

    def back_local(tile):
        source_ref, target_ref = back_ends(tile, me_c)
        return pltpu.make_async_copy(source_ref, target_ref, back_own.at[tile])

    def collect_tile(tile, early):
        for s in range(FOLD):
            collect(FOLD * tile + s, tile, s)
        for h in range(2):
            r_rows[tile, pl.ds(h, 128, stride=2), :] = p_buf[tile, h].T
        if early:
            for r in range(1, NC):
                back_copy(tile, r).start()
            back_local(tile).start()
        else:
            third_send_all(tile, False)

    def back_tile_on(tile):
        cross_many(z_buf, tile, back_recv).wait()
        back_local(tile).wait()
        third_send_all(tile, True)

    for part in range(len(PARTS)):
        for copy in second_halos(part):
            copy.wait()
        sweep_y_of(1, SECOND_HALOS[part], outer)
    theta_outer(1, 0, ND)

    def collect_some(low, high, early):
        def body(tile, carry):
            collect_tile(tile, early)
            return carry

        lax.fori_loop(low, high, body, 0)

    def back_on(tile, carry):
        back_tile_on(tile)
        return carry

    collect_some(EARLY, EARLY + 1, False)
    collect(LAST, range(EARLY), None)
    collect_some(0, EARLY, True)
    collect_some(EARLY + 1, TILES, False)
    lax.fori_loop(0, EARLY, back_on, 0)

    def put(direction, parts, early):
        for u in range(6):
            at = own_put_at[u] if early else put_at[u]
            which = own_put_tile[u] if early else put_tile[u]
            value = jnp.zeros((8, 128), jnp.float32)
            for v in range(TILES):
                if u in SLOT_TILES[v]:
                    value = jnp.where(which == v, lanes(parts[v], at), value)
            columns = pl.ds(128 * u, 128)
            if early:
                out[direction, :, columns] = value
            else:
                o_buf[direction, :, columns] = value

    def fourth_ends(k, peer):
        part = chunk(k)
        return o_buf.at[part, slot_of(peer), :], out.at[part, me_c, :]

    def fourth_copy(k, r):
        peer = (me_c + r) % NC
        source_ref, target_ref = fourth_ends(k, peer)
        return pltpu.make_async_remote_copy(
            src_ref=source_ref,
            dst_ref=target_ref,
            send_sem=fourth_send.at[k],
            recv_sem=fourth_recv.at[k],
            device_id={"comp": peer, "lat": me_l},
            device_id_type=pl.DeviceIdType.MESH,
        )

    def fourth_local(k):
        source_ref, target_ref = fourth_ends(k, me_c)
        return pltpu.make_async_copy(source_ref, target_ref, fourth_own.at[k])

    def fourth_send_all(k):
        for r in range(1, NC):
            fourth_copy(k, r).start()
        fourth_local(k).start()

    def put_tile_of(early):
        def body(tile, carry):
            many(n_buf, tile, third_recv).wait()
            third_local(tile, early).wait()
            swapped = []
            for v in range(TILES):
                parts = [n_buf[tile, min(FOLD * v + b, NL - 1)] for b in range(FOLD)]
                swapped.append(swap_blocks(parts, block_masks, turns))
            for s in range(FOLD):
                put(FOLD * tile + s, [swapped[v][s] for v in range(TILES)], early)
            if not early:
                fourth_send_all(tile)
            return carry

        return body

    def put_last():
        parts = []
        spare = 120 + (lane & 7)
        for v in range(TILES):
            value = jnp.zeros((8, 128), jnp.float32)
            for b in range(FOLD):
                if FOLD * v + b < NL:
                    for e in range(3):
                        got = lanes(n_buf[e, FOLD * v + b], spare)
                        value = jnp.where((lane >> 3) == 3 * b + e, got, value)
            parts.append(value)
        put(LAST, parts, True)

    lax.fori_loop(EARLY, TILES, put_tile_of(False), 0)
    lax.fori_loop(0, EARLY, put_tile_of(True), 0)
    put_last()

    for g in range(EARLY, TILES):
        first_wait(g, first_send).wait()
    for tile in range(TILES):
        many(r_buf, tile, second_send).wait()
        many(n_buf, tile, third_send).wait()
    for tile in range(EARLY):
        cross_many(r_buf, tile, cross_send).wait()
        cross_many(z_buf, tile, back_send).wait()
    for k in range(EARLY, TILES):
        fourth_local(k).wait()
        part = out.at[chunk(k), pl.ds(0, NC - 1), :]
        pltpu.make_async_copy(part, part, fourth_recv.at[k]).wait()
        pltpu.make_async_copy(part, part, fourth_send.at[k]).wait()


def per_device(spectra_in, group_speed, turn_rate, sea_mask, sea_cell, slab_counts):
    f32 = jnp.float32
    vreg = (8, 128)
    dma = pltpu.SemaphoreType.DMA
    hbm = pl.BlockSpec(memory_space=pltpu.HBM)
    return pl.pallas_call(
        kernel,
        out_shape=pltpu.VMEM((ND, NC, SLOTS), f32),
        in_specs=[hbm] * 6,
        out_specs=pl.BlockSpec(memory_space=pltpu.VMEM),
        scratch_shapes=[
            pltpu.VMEM((1, ROWS, 1024), f32),
            pltpu.VMEM((1, ROWS, 1024), f32),
            pltpu.VMEM((ROWS, 1024), jnp.int32),
            pltpu.VMEM((48, 128), jnp.int32),
            pltpu.SMEM((NL,), jnp.int32),
            pltpu.SMEM((2, ND), f32),
            dma((7,)),
            pltpu.VMEM((ND, NC, SLOTS), f32),
            pltpu.VMEM((ND, NC, SLOTS), f32),
            pltpu.VMEM((NL, TILES) + vreg, f32),
            pltpu.VMEM((EARLY, NL) + vreg, f32),
            pltpu.VMEM((TILES, NL) + vreg, f32),
            pltpu.VMEM((TILES, 2, 128, 128), f32),
            pltpu.VMEM((EARLY, NL) + vreg, f32),
            pltpu.VMEM((TILES, NL) + vreg, f32),
            pltpu.VMEM((ND, NC, SLOTS), f32),
            pltpu.VMEM((2, ND, ROWS + 4) + vreg, f32),
            pltpu.VMEM((ND, ROWS) + vreg, f32),
            pltpu.VMEM((ND, ROWS) + vreg, f32),
            pltpu.VMEM((64, 128), f32),
            pltpu.VMEM((64, 128), f32),
            pltpu.VMEM((64, 128), f32),
            pltpu.VMEM((4,) + vreg, f32),
            pltpu.VMEM((ROWS,) + vreg, f32),
            pltpu.VMEM((ROWS + 1,) + vreg, f32),
            pltpu.VMEM((TILES,) + vreg, jnp.int32),
            pltpu.VMEM((TILES,) + vreg, jnp.int32),
            pltpu.VMEM((6,) + vreg, jnp.int32),
            pltpu.VMEM((6,) + vreg, jnp.int32),
            pltpu.VMEM((6,) + vreg, jnp.int32),
            pltpu.VMEM((6,) + vreg, jnp.int32),
            pltpu.VMEM((ROWS,) + vreg, jnp.int32),
            pltpu.VMEM((ROWS,) + vreg, jnp.int32),
            pltpu.VMEM((ROWS,) + vreg, jnp.int32),
            pltpu.VMEM((ROWS,) + vreg, jnp.int32),
            pltpu.VMEM((3, 2) + vreg, jnp.int32),
            pltpu.VMEM((3, 2) + vreg, jnp.int32),
            pltpu.VMEM((TILES,) + vreg, f32),
            dma((TILES,)), dma((TILES,)), dma((TILES,)),
            dma((TILES,)), dma((TILES,)), dma((TILES,)),
            dma((EARLY,)), dma((EARLY,)), dma((EARLY,)),
            dma((EARLY,)), dma((EARLY,)), dma((EARLY,)),
            dma((4,)), dma((4,)), dma((2, HALOS)), dma((2, HALOS)),
            dma((TILES,)), dma((TILES,)), dma((TILES,)),
            dma((TILES,)), dma((TILES,)), dma((TILES,)),
        ],
        compiler_params=pltpu.CompilerParams(
            collective_id=0, has_side_effects=True, vmem_limit_bytes=64000 * 1024
        ),
        name="wave_step",
    )(
        spectra_in.transpose(1, 0, 2),
        group_speed,
        turn_rate,
        sea_mask,
        sea_cell.reshape(48, 128),
        slab_counts,
    ).transpose(1, 0, 2)


def solution(mesh):
    in_specs = (
        P(None, None, ("comp", "lat")),
        P("comp", "lat", None),
        P("comp", "lat", None),
        P("lat", None),
        P("lat"),
        P(),
    )
    out_specs = P(None, None, ("comp", "lat"))
    return jax.shard_map(
        per_device, mesh=mesh, in_specs=in_specs, out_specs=out_specs, check_vma=False
    )
```

```python
import math

import jax
import jax.numpy as jnp
import numpy as np
from jax import lax
from jax.experimental import pallas as pl
from jax.experimental.pallas import tpu as pltpu
from jax.sharding import PartitionSpec as P

NC = 8
NL = 32
ND = 36
SLOTS = 768
BUCKET = 24
ROWS = 8
FOLD = 5
TILES = 7
EARLY = 3
LAST = ND - 1
PARTS = ((0, 12), (12, 12), (24, 12))
BEFORE = ((34, 16), (14, 12), (26, 8))
ORDER = (4, 3, 2, 1, 8, 12, 5, 6, 7, 16, 20, 11, 10, 9, 24, 28, 13, 14, 15, 19, 18, 17, 21, 22, 23, 27, 26, 25, 29, 30, 31)
SIN_POS = 19

ANGLES = np.arange(ND, dtype=np.float32) * np.float32(2.0 * math.pi / ND)
COS = np.cos(ANGLES).astype(np.float32)
SIN = np.sin(ANGLES).astype(np.float32)
TURN = (0.5 * (COS + np.roll(COS, -1))).astype(np.float32)
assert (SIN[:SIN_POS] >= 0).all() and (SIN[SIN_POS:] < 0).all()

SLOT_TILES = ((0,), (0, 1), (0, 1, 2), (1, 2, 3), (1, 2, 3, 4), (2, 3, 4, 5), (2, 3, 4, 5))
POINT_TILES = tuple(
    tuple(range(max(0, 4 * v - 20) // 8, min(2, (4 * v + 3) // 8) + 1)) for v in range(ROWS)
)
ROW_TILES = tuple(tuple(range(2 * u, min(7, 2 * u + 6) + 1)) for u in range(3))


def ranges(first, number):
    cuts = []
    for j in range(first, first + number):
        j = j % ND
        if cuts and j == cuts[-1][0] + cuts[-1][1] and j not in (0, SIN_POS):
            cuts[-1][1] += 1
        else:
            cuts.append([j, 1])
    return [(low, size, low < SIN_POS) for low, size in cuts]


SECOND_HALOS = [ranges(*p) for p in PARTS]
HALOS = 2 * (TILES + 1)
assert sum(len(r) for r in SECOND_HALOS) <= TILES + 1


def lanes(values, index):
    return jnp.take_along_axis(values, index, axis=1)


def sublanes(values, index):
    return jnp.take_along_axis(values, index, axis=0)


def iotas():
    return (
        lax.broadcasted_iota(jnp.int32, (8, 128), 0),
        lax.broadcasted_iota(jnp.int32, (8, 128), 1),
    )


def swap_blocks(parts, block_masks, turns):
    rolled = []
    for k in range(FOLD):
        diagonal = parts[(FOLD - 1 + k) % FOLD]
        for b in range(FOLD - 1):
            diagonal = jnp.where(block_masks[b], parts[(b + k) % FOLD], diagonal)
        rolled.append(diagonal if k == 0 else lanes(diagonal, turns[k]))
    outs = []
    for a in range(FOLD):
        value = rolled[(FOLD - 1 - a) % FOLD]
        for b in range(FOLD - 1):
            value = jnp.where(block_masks[b], rolled[(b - a) % FOLD], value)
        outs.append(value)
    return outs


def flux(q, d, curvature, c):
    sixth = 1.0 / 6.0
    return c * (q + (1.0 - c) * (0.5 * d - (c * sixth + sixth) * curvature))


def sweep_x(q, c, sign, sub, lane):
    east = lanes(q, (lane + 1) & 127)
    east = jnp.where(lane == 127, sublanes(east, (sub + 1) & 7), east)
    east = jnp.where((lane == 127) & (sub == 7), 0.0, east)
    d = east - q
    side = lanes(d, (lane - sign) & 127)
    edge = lane == jnp.where(sign > 0, 0, 127)
    side = jnp.where(edge, sublanes(side, (sub - sign) & 7), side)
    side = jnp.where(edge & (sub == jnp.where(sign > 0, 0, 7)), q, side)
    curvature = (d - side) * jnp.where(sign > 0, 1.0, -1.0)
    f = flux(q, d, curvature, c)
    west = lanes(f, (lane - 1) & 127)
    west = jnp.where(lane == 0, sublanes(west, (sub - 1) & 7), west)
    return q - (f - west)


def kernel(
    spectra, speed_in, turn_in, mask_in, cells_in, counts_in, out,
    speed, turn, mask, cells, counts, trig, load_sem,
    a_buf, own_buf, m_buf, x_buf, r_buf, p_buf, z_buf, n_buf, o_buf, x_ext, y_buf, done,
    spd, trn, msk, stat_halo, sx, sy,
    pack_at, own_at, put_at, put_tile, own_put_at, own_put_tile, row_at, row_tile, lane_at, take_at, back_row, back_tile, w_last,
    first_send, first_recv, first_own, second_send, second_recv, second_own,
    cross_send, cross_recv, cross_own, back_send, back_recv, back_own,
    stat_send, stat_recv, halo_send, halo_recv,
    third_send, third_recv, third_own, fourth_send, fourth_recv, fourth_own,
):
    me_c = lax.axis_index("comp")
    me_l = lax.axis_index("lat")
    sub, lane = iotas()

    def slot_of(c):
        return (c % 4) * 2 + c // 4

    loads = [
        pltpu.make_async_copy(source_ref, target_ref, load_sem.at[k])
        for k, (source_ref, target_ref) in enumerate(
            (
                (counts_in, counts),
                (spectra.at[pl.ds(0, FOLD * EARLY)], own_buf.at[pl.ds(0, FOLD * EARLY)]),
                (spectra.at[pl.ds(LAST, 1)], own_buf.at[pl.ds(LAST, 1)]),
                (speed_in, speed),
                (turn_in, turn),
                (mask_in, mask),
                (cells_in, cells),
            )
        )
    ]
    for load in loads:
        load.start()

    def chunk(tile):
        return pl.ds(FOLD * tile, FOLD)

    def first_ends(g, peer):
        return spectra.at[chunk(g), peer, :], a_buf.at[chunk(g), slot_of(me_c), :]

    def first_local(g):
        source_ref, target_ref = first_ends(g, me_c)
        return pltpu.make_async_copy(source_ref, target_ref, first_own.at[g])

    for g in range(EARLY, TILES):
        first_local(g).start()

    barrier = pltpu.get_barrier_semaphore()

    def greet_comp(r, carry):
        pl.semaphore_signal(
            barrier, inc=1, device_id={"comp": (me_c + r) % NC, "lat": me_l}, device_id_type=pl.DeviceIdType.MESH
        )
        return carry

    def greet_lat(r, carry):
        pl.semaphore_signal(
            barrier, inc=1, device_id={"comp": me_c, "lat": (me_l + r) % NL}, device_id_type=pl.DeviceIdType.MESH
        )
        return carry

    lax.fori_loop(1, NC, greet_comp, 0)
    lax.fori_loop(1, NL, greet_lat, 0)

    for j in range(ND):
        trig[0, j] = jnp.float32(float(COS[j]))
        trig[1, j] = jnp.float32(float(SIN[j]))

    for load in loads:
        load.wait()
    starts = [jnp.int32(0)]
    for slab in range(NL):
        starts.append(starts[-1] + counts[slab])
    own_start = jnp.int32(0)
    for slab in range(NL):
        own_start = own_start + jnp.where(slab < me_l, counts[slab], 0)

    source = ((sub & 1) * 4 + (sub >> 1)) * NL + me_l
    own_source = me_c * NL + me_l
    block = (lane * 171) >> 12
    in_block = lane - block * BUCKET
    block_masks = [block == b for b in range(FOLD)]
    turns = [None] + [
        jnp.where(lane >= BUCKET * k, lane - BUCKET * k, lane - BUCKET * k + BUCKET * FOLD) & 127
        for k in range(1, FOLD)
    ]
    for v in range(TILES):
        base = jnp.full((8, 128), starts[min(FOLD * v, NL - 1)], jnp.int32)
        for b in range(1, FOLD):
            if FOLD * v + b < NL:
                base = jnp.where(block == b, starts[FOLD * v + b], base)
        pack_at[v] = ((base - source + 255) >> 8) + in_block
        own_at[v] = ((base - own_source + 255) >> 8) + in_block

    for t in range(8):
        columns = pl.ds(128 * t, 128)
        spd[pl.ds(t, 8, stride=8), :] = speed[0, :, columns]
        trn[pl.ds(t, 8, stride=8), :] = turn[0, :, columns]
        msk[pl.ds(t, 8, stride=8), :] = mask[:, columns].astype(jnp.float32)

    for u in range(6):
        for origin, at, which in ((source, put_at, put_tile), (own_source, own_put_at, own_put_tile)):
            point = origin + (lane + 128 * u) * 256
            slab = jnp.zeros((8, 128), jnp.int32)
            begin = jnp.zeros((8, 128), jnp.int32)
            for s in range(1, NL + 1):
                past = point >= starts[s]
                slab = jnp.where(past, s, slab)
                begin = jnp.where(past, starts[s], begin)
            nth = lane + 128 * u - ((begin - origin + 255) >> 8)
            tile = (slab * 205) >> 10
            at[u] = ((slab - tile * FOLD) * BUCKET + nth) & 127
            which[u] = jnp.where(slab < NL, tile, -1)

    ones = jnp.ones((128, 128), jnp.bfloat16)
    deep = lax.broadcasted_iota(jnp.int32, (128, 128), 0)
    wide = lax.broadcasted_iota(jnp.int32, (128, 128), 1)
    before = jnp.where(deep < wide, 1.0, 0.0).astype(jnp.bfloat16)
    above = jnp.where(wide < deep, 1.0, 0.0).astype(jnp.bfloat16)[:64, :64]
    sea = msk[...].astype(jnp.bfloat16)
    inside = jnp.dot(sea, before, preferred_element_type=jnp.float32)
    totals = jnp.dot(sea, ones, preferred_element_type=jnp.float32)
    offsets = jnp.dot(above, totals.astype(jnp.bfloat16), preferred_element_type=jnp.float32)
    inside = inside.astype(jnp.int32)
    offsets = offsets.astype(jnp.int32)
    low_source = (lane & 3) * NL + (lane >> 2)
    for v in range(ROWS):
        offset = offsets[8 * v : 8 * v + 8]
        point = offset + inside[8 * v : 8 * v + 8] + own_start
        lane_at[v] = ((point & 31) << 2) | ((point >> 5) & 3)
        point = offset + ((low_source - own_start - offset) & 127)
        row_at[v] = (point >> 8) & 7
        row_tile[v] = ((point >> 11) << 1) + (((point + own_start) >> 7) & 1)
    cell_at = []
    for u in range(3):
        even = cells[pl.ds(16 * u, 8, stride=2), :]
        odd = cells[pl.ds(16 * u + 1, 8, stride=2), :]
        for h in range(2):
            rho = (low_source + 128 * h - own_start) & 255
            cell = jnp.where(rho < 128, lanes(even, rho & 127), lanes(odd, rho & 127))
            cell_at.append(cell)
            back_row[u, h] = (cell >> 7) & 7
            back_tile[u, h] = cell >> 10
    for v in range(ROWS):
        index = row_at[v]
        which = row_tile[v]
        value = jnp.zeros((8, 128), jnp.int32)
        for u in POINT_TILES[v]:
            for h in range(2):
                value = jnp.where(which == 2 * u + h, sublanes(cell_at[2 * u + h], index), value)
        take_at[v] = value & 127

    for v in range(ROWS):
        rows = pl.ds(8 * v, 8)
        s = spd[rows, :]
        m = msk[rows, :]

        def eastward(x):
            east = lanes(x, (lane + 1) & 127)
            return jnp.where(lane == 127, sublanes(east, (sub + 1) & 7), east)

        face = 0.5 * (s + eastward(s)) * m * eastward(m)
        sx[v] = jnp.where((lane == 127) & (sub == 7), 0.0, face)
        trn[rows, :] = trn[rows, :] * m
        if v < ROWS - 1:
            after = pl.ds(8 * v + 8, 8)
            sy[v + 1] = 0.5 * (s + spd[after, :]) * m * msk[after, :]
    def slot_rows(buffer, direction):
        return [buffer[direction, :, pl.ds(128 * u, 128)] for u in range(6)]

    def windows(at_ref, v, rows):
        at = at_ref[v]
        low = at & 127
        value = None
        for u in SLOT_TILES[v]:
            got = lanes(rows[u], low)
            value = got if value is None else jnp.where((at >> 7) == u, got, value)
        return value

    def pack(tile, early):
        buffer, at_ref = (own_buf, own_at) if early else (a_buf, pack_at)
        rows = [slot_rows(buffer, FOLD * tile + s) for s in range(FOLD)]
        for v in range(TILES):
            parts = [windows(at_ref, v, rows[s]) for s in range(FOLD)]
            for b, value in enumerate(swap_blocks(parts, block_masks, turns)):
                if FOLD * v + b < NL:
                    if early:
                        extra = lanes(w_last[v], BUCKET * b + 8 * tile + (lane & 7))
                        value = jnp.where(lane >= 120, extra, value)
                    m_buf[FOLD * v + b, tile] = value

    def pack_early(tile, carry):
        pack(tile, True)
        return carry

    last_rows = slot_rows(own_buf, LAST)
    for v in range(TILES):
        w_last[v] = windows(own_at, v, last_rows)
    lax.fori_loop(0, EARLY, pack_early, 0)

    pl.semaphore_wait(barrier, NC - 1 + NL - 1)

    def first_wait(g, sem):
        ref = a_buf.at[chunk(g), pl.ds(0, NC - 1), :]
        return pltpu.make_async_copy(ref, ref, sem.at[g])

    def first_copy(g, r):
        peer = (me_c + r) % NC
        source_ref, target_ref = first_ends(g, peer)
        return pltpu.make_async_remote_copy(
            src_ref=source_ref,
            dst_ref=target_ref,
            send_sem=first_send.at[g],
            recv_sem=first_recv.at[g],
            device_id={"comp": peer, "lat": me_l},
            device_id_type=pl.DeviceIdType.MESH,
        )


    north = {"comp": me_c, "lat": (me_l + 1) % NL}
    south = {"comp": me_c, "lat": (me_l + NL - 1) % NL}

    def stat_copy(k):
        ref = (spd, msk)[k % 2]
        row = 56 if k < 2 else 0
        return pltpu.make_async_remote_copy(
            src_ref=ref.at[pl.ds(row, 8), :],
            dst_ref=stat_halo.at[k],
            send_sem=stat_send.at[k],
            recv_sem=stat_recv.at[k],
            device_id=north if k < 2 else south,
            device_id_type=pl.DeviceIdType.MESH,
        )


    def second_copy(tile, r, early):
        peer = (me_l + r) % NL
        return pltpu.make_async_remote_copy(
            src_ref=m_buf.at[peer, tile],
            dst_ref=x_buf.at[tile, me_l] if early else r_buf.at[tile, me_l],
            send_sem=second_send.at[tile],
            recv_sem=second_recv.at[tile],
            device_id={"comp": me_c, "lat": peer},
            device_id_type=pl.DeviceIdType.MESH,
        )

    def second_local(tile, early):
        return pltpu.make_async_copy(
            m_buf.at[me_l, tile],
            x_buf.at[tile, me_l] if early else r_buf.at[tile, me_l],
            second_own.at[tile],
        )

    def many(ref, tile, sem):
        part = ref.at[tile, pl.ds(0, NL - 1)]
        return pltpu.make_async_copy(part, part, sem.at[tile])

    def send_tile(early):
        def body(tile, carry):
            if not early:
                first_wait(tile, first_recv).wait()
                first_local(tile).wait()
                pack(tile, False)
            for r in ORDER:
                second_copy(tile, r, early).start()
            second_local(tile, early).start()
            return carry

        return body

    for g in range(EARLY, TILES):
        for r in range(1, NC):
            first_copy(g, r).start()
    for k in range(4):
        stat_copy(k).start()
    lax.fori_loop(0, EARLY, send_tile(True), 0)
    lax.fori_loop(EARLY, TILES, send_tile(False), 0)

    def cross_ends(tile, peer):
        return x_buf.at[tile, :, peer, :], r_buf.at[tile, :, slot_of(me_c), :]

    def cross_copy(tile, r):
        peer = (me_c + r) % NC
        source_ref, target_ref = cross_ends(tile, peer)
        return pltpu.make_async_remote_copy(
            src_ref=source_ref,
            dst_ref=target_ref,
            send_sem=cross_send.at[tile],
            recv_sem=cross_recv.at[tile],
            device_id={"comp": peer, "lat": me_l},
            device_id_type=pl.DeviceIdType.MESH,
        )

    def cross_local(tile):
        source_ref, target_ref = cross_ends(tile, me_c)
        return pltpu.make_async_copy(source_ref, target_ref, cross_own.at[tile])

    def cross_many(ref, tile, sem):
        part = ref.at[tile, :, pl.ds(0, NC - 1), :]
        return pltpu.make_async_copy(part, part, sem.at[tile])

    def cross_tile(tile, carry):
        many(x_buf, tile, second_recv).wait()
        second_local(tile, True).wait()
        for r in range(1, NC):
            cross_copy(tile, r).start()
        cross_local(tile).start()
        return carry

    lax.fori_loop(0, EARLY, cross_tile, 0)

    for k in range(4):
        stat_copy(k).wait()
    south_mask = jnp.where(me_l > 0, stat_halo[1], 0.0)
    north_mask = jnp.where(me_l < NL - 1, stat_halo[3], 0.0)
    sy[0] = 0.5 * (stat_halo[0] + spd[0:8, :]) * south_mask * msk[0:8, :]
    sy[8] = 0.5 * (stat_halo[2] + spd[56:64, :]) * north_mask * msk[56:64, :]

    r_rows = r_buf.reshape(TILES, NL * 8, 128)

    def turn_points(tile, early):
        if early:
            cross_many(r_buf, tile, cross_recv).wait()
            cross_local(tile).wait()
        else:
            many(r_buf, tile, second_recv).wait()
            second_local(tile, False).wait()
        for h in range(2):
            p_buf[tile, h] = r_rows[tile, pl.ds(h, 128, stride=2), :].T

    def point_ref(tile, s, u, h):
        if s is None:
            return p_buf.at[tile[u], h, pl.ds(120, 8), :]
        return p_buf.at[tile, h, pl.ds(pl.multiple_of(BUCKET * s + 8 * u, 8), 8), :]

    def place(direction, tile, s):
        held = {(u, h): point_ref(tile, s, u, h)[...] for u in range(3) for h in range(2)}
        cosine = trig[0, direction]
        sign = jnp.where(cosine >= 0.0, 1, -1)
        for v in range(ROWS):
            index = row_at[v]
            which = row_tile[v]
            value = None
            for u in POINT_TILES[v]:
                for h in range(2):
                    got = sublanes(held[u, h], index)
                    value = got if value is None else jnp.where(which == 2 * u + h, got, value)
            q = jnp.where(msk[pl.ds(8 * v, 8), :] > 0.0, lanes(value, lane_at[v]), 0.0)
            x_ext[0, direction, v + 2] = sweep_x(q, cosine * sx[v], sign, sub, lane)

    def halo_copy(step, dirs, rows, to_north, k):
        source_row = 2 + ROWS - rows if to_north else 2
        target_row = 2 - rows if to_north else 2 + ROWS
        return pltpu.make_async_remote_copy(
            src_ref=x_ext.at[step, dirs, pl.ds(source_row, rows)],
            dst_ref=x_ext.at[step, dirs, pl.ds(target_row, rows)],
            send_sem=halo_send.at[step, k],
            recv_sem=halo_recv.at[step, k],
            device_id=north if to_north else south,
            device_id_type=pl.DeviceIdType.MESH,
        )

    def tile_halos(tile, kind):
        north_rows, south_rows = ((2, 1), (2, 2), (1, 2))[kind]
        dirs = pl.ds(FOLD * tile, 1 if isinstance(tile, int) and tile == TILES else FOLD)
        return (
            halo_copy(0, dirs, north_rows, True, 2 * tile),
            halo_copy(0, dirs, south_rows, False, 2 * tile + 1),
        )

    def second_halos(part):
        k = 2 * sum(len(r) for r in SECOND_HALOS[:part])
        copies = []
        for low, size, positive in SECOND_HALOS[part]:
            dirs = pl.ds(low, size)
            copies.append(halo_copy(1, dirs, 2 if positive else 1, True, k))
            copies.append(halo_copy(1, dirs, 1 if positive else 2, False, k + 1))
            k += 2
        return copies

    def sweep_y(step, direction, positive, row_list):
        sine = trig[1, direction]

        def row(r):
            value = x_ext[step, direction, r + 2]
            if r < 0:
                value = jnp.where(me_l > 0, value, 0.0)
            if r >= ROWS:
                value = jnp.where(me_l < NL - 1, value, 0.0)
            return value

        diffs = {}
        fluxes = {}

        def diff(f):
            if f not in diffs:
                diffs[f] = row(f) - row(f - 1)
            return diffs[f]

        def face(f):
            if f not in fluxes:
                if positive:
                    curvature = diff(f) - diff(f - 1)
                else:
                    curvature = diff(f + 1) - diff(f)
                fluxes[f] = flux(row(f - 1), diff(f), curvature, sine * sy[f])
            return fluxes[f]

        for r in row_list:
            y_buf[direction, r] = row(r) - (face(r + 1) - face(r))

    def sweep_y_of(step, cuts, row_list):
        for low, size, positive in cuts:

            def body(direction, carry, positive=positive):
                sweep_y(step, direction, positive, row_list)
                return carry

            lax.fori_loop(low, low + size, body, 0)

    def sweep_theta(step, first, number, r):
        t = trn[pl.ds(pl.multiple_of(8 * r, 8), 8), :]
        forward = t >= 0.0
        q = {k: y_buf[k % ND, r] for k in range(first - 2, first + number + 2)}
        d = {k: q[k + 1] - q[k] for k in range(first - 2, first + number + 1)}

        def face(k):
            ahead = d[k + 1] - d[k]
            behind = d[k] - d[k - 1]
            turning = float(TURN[k % ND])
            if turning >= 0:
                curvature = jnp.where(forward, behind, ahead)
            else:
                curvature = jnp.where(forward, ahead, behind)
            return flux(q[k], d[k], curvature, turning * t)

        prior = face(first - 1)
        for k in range(first, first + number):
            f = face(k)
            value = q[k] - (f - prior)
            prior = f
            j = k % ND
            if step == 0:
                sign = 1 if COS[j] >= 0 else -1
                x_ext[1, j, r + 2] = sweep_x(value, float(COS[j]) * sx[r], sign, sub, lane)
            else:
                done[j, r] = value

    inner = tuple(range(2, 6))
    outer = (0, 1, 6, 7)

    def theta_inner(step):
        def body(r, carry):
            sweep_theta(step, 0, ND, r)
            return carry

        lax.fori_loop(2, 6, body, 0)

    def theta_outer(step, first, number):
        def body(k, carry):
            for r in outer:
                sweep_theta(step, first, number, r)
            return carry

        lax.fori_loop(0, 1, body, 0)

    def receive_tile(kind):
        def body(tile, carry):
            turn_points(tile, kind == 0)
            for s in range(FOLD):
                place(FOLD * tile + s, tile, s)
            for copy in tile_halos(tile, kind):
                copy.start()
            for s in range(FOLD):
                positive = kind == 0 or (kind == 1 and FOLD * tile + s < SIN_POS)
                sweep_y(0, FOLD * tile + s, positive, inner)
            return carry

        return body

    middle = SIN_POS // FOLD
    assert middle == EARLY
    lax.fori_loop(0, middle, receive_tile(0), 0)
    place(LAST, range(EARLY), None)
    for copy in tile_halos(TILES, 2):
        copy.start()
    sweep_y(0, LAST, False, inner)
    receive_tile(1)(middle, 0)
    lax.fori_loop(middle + 1, TILES, receive_tile(2), 0)

    theta_inner(0)
    for tile in range(TILES + 1):
        for copy in tile_halos(tile, 0 if tile < middle else 1 if tile == middle else 2):
            copy.wait()
    for part in range(len(PARTS)):
        sweep_y_of(0, ranges(*BEFORE[part]), outer)
        theta_outer(0, *PARTS[part])
        for copy in second_halos(part):
            copy.start()
    sweep_y_of(1, ranges(0, ND), inner)
    theta_inner(1)

    def collect(direction, tile, s):
        taken = [lanes(done[direction, v], take_at[v]) for v in range(ROWS)]
        for u in range(3):
            for h in range(2):
                index = back_row[u, h]
                which = back_tile[u, h]
                value = None
                for v in ROW_TILES[u]:
                    got = sublanes(taken[v], index)
                    value = got if value is None else jnp.where(which == v, got, value)
                point_ref(tile, s, u, h)[...] = value

    def third_ends(tile, peer, early):
        source_ref = z_buf.at[tile, peer] if early else r_buf.at[tile, peer]
        return source_ref, n_buf.at[tile, me_l]

    def third_copy(tile, r, early):
        peer = (me_l + r) % NL
        source_ref, target_ref = third_ends(tile, peer, early)
        return pltpu.make_async_remote_copy(
            src_ref=source_ref,
            dst_ref=target_ref,
            send_sem=third_send.at[tile],
            recv_sem=third_recv.at[tile],
            device_id={"comp": me_c, "lat": peer},
            device_id_type=pl.DeviceIdType.MESH,
        )

    def third_local(tile, early):
        source_ref, target_ref = third_ends(tile, me_l, early)
        return pltpu.make_async_copy(source_ref, target_ref, third_own.at[tile])

    def third_send_all(tile, early):
        for r in ORDER:
            third_copy(tile, r, early).start()
        third_local(tile, early).start()

    def back_ends(tile, peer):
        return r_buf.at[tile, :, slot_of(peer), :], z_buf.at[tile, :, me_c, :]

    def back_copy(tile, r):
        peer = (me_c + r) % NC
        source_ref, target_ref = back_ends(tile, peer)
        return pltpu.make_async_remote_copy(
            src_ref=source_ref,
            dst_ref=target_ref,
            send_sem=back_send.at[tile],
            recv_sem=back_recv.at[tile],
            device_id={"comp": peer, "lat": me_l},
            device_id_type=pl.DeviceIdType.MESH,
        )

    def back_local(tile):
        source_ref, target_ref = back_ends(tile, me_c)
        return pltpu.make_async_copy(source_ref, target_ref, back_own.at[tile])

    def collect_tile(tile, early):
        for s in range(FOLD):
            collect(FOLD * tile + s, tile, s)
        for h in range(2):
            r_rows[tile, pl.ds(h, 128, stride=2), :] = p_buf[tile, h].T
        if early:
            for r in range(1, NC):
                back_copy(tile, r).start()
            back_local(tile).start()
        else:
            third_send_all(tile, False)

    def back_tile_on(tile):
        cross_many(z_buf, tile, back_recv).wait()
        back_local(tile).wait()
        third_send_all(tile, True)

    for part in range(len(PARTS)):
        for copy in second_halos(part):
            copy.wait()
        sweep_y_of(1, SECOND_HALOS[part], outer)
    theta_outer(1, 0, ND)

    def collect_some(low, high, early):
        def body(tile, carry):
            collect_tile(tile, early)
            return carry

        lax.fori_loop(low, high, body, 0)

    def back_on(tile, carry):
        back_tile_on(tile)
        return carry

    collect_some(EARLY, EARLY + 1, False)
    collect(LAST, range(EARLY), None)
    collect_some(0, EARLY, True)
    collect_some(EARLY + 1, TILES, False)
    lax.fori_loop(0, EARLY, back_on, 0)

    def put(direction, parts, early):
        for u in range(6):
            at = own_put_at[u] if early else put_at[u]
            which = own_put_tile[u] if early else put_tile[u]
            value = jnp.zeros((8, 128), jnp.float32)
            for v in range(TILES):
                if u in SLOT_TILES[v]:
                    value = jnp.where(which == v, lanes(parts[v], at), value)
            columns = pl.ds(128 * u, 128)
            if early:
                out[direction, :, columns] = value
            else:
                o_buf[direction, :, columns] = value

    def fourth_ends(k, peer):
        part = chunk(k)
        return o_buf.at[part, slot_of(peer), :], out.at[part, me_c, :]

    def fourth_copy(k, r):
        peer = (me_c + r) % NC
        source_ref, target_ref = fourth_ends(k, peer)
        return pltpu.make_async_remote_copy(
            src_ref=source_ref,
            dst_ref=target_ref,
            send_sem=fourth_send.at[k],
            recv_sem=fourth_recv.at[k],
            device_id={"comp": peer, "lat": me_l},
            device_id_type=pl.DeviceIdType.MESH,
        )

    def fourth_local(k):
        source_ref, target_ref = fourth_ends(k, me_c)
        return pltpu.make_async_copy(source_ref, target_ref, fourth_own.at[k])

    def fourth_send_all(k):
        for r in range(1, NC):
            fourth_copy(k, r).start()
        fourth_local(k).start()

    def put_tile_of(early):
        def body(tile, carry):
            many(n_buf, tile, third_recv).wait()
            third_local(tile, early).wait()
            swapped = []
            for v in range(TILES):
                parts = [n_buf[tile, min(FOLD * v + b, NL - 1)] for b in range(FOLD)]
                swapped.append(swap_blocks(parts, block_masks, turns))
            for s in range(FOLD):
                put(FOLD * tile + s, [swapped[v][s] for v in range(TILES)], early)
            if not early:
                fourth_send_all(tile)
            return carry

        return body

    def put_last():
        parts = []
        spare = 120 + (lane & 7)
        for v in range(TILES):
            value = jnp.zeros((8, 128), jnp.float32)
            for b in range(FOLD):
                if FOLD * v + b < NL:
                    for e in range(3):
                        got = lanes(n_buf[e, FOLD * v + b], spare)
                        value = jnp.where((lane >> 3) == 3 * b + e, got, value)
            parts.append(value)
        put(LAST, parts, True)

    lax.fori_loop(EARLY, TILES, put_tile_of(False), 0)
    lax.fori_loop(0, EARLY, put_tile_of(True), 0)
    put_last()

    for g in range(EARLY, TILES):
        first_wait(g, first_send).wait()
    for tile in range(TILES):
        many(r_buf, tile, second_send).wait()
        many(n_buf, tile, third_send).wait()
    for tile in range(EARLY):
        cross_many(r_buf, tile, cross_send).wait()
        cross_many(z_buf, tile, back_send).wait()
    for k in range(EARLY, TILES):
        fourth_local(k).wait()
        part = out.at[chunk(k), pl.ds(0, NC - 1), :]
        pltpu.make_async_copy(part, part, fourth_recv.at[k]).wait()
        pltpu.make_async_copy(part, part, fourth_send.at[k]).wait()


def per_device(spectra_in, group_speed, turn_rate, sea_mask, sea_cell, slab_counts):
    f32 = jnp.float32
    vreg = (8, 128)
    dma = pltpu.SemaphoreType.DMA
    hbm = pl.BlockSpec(memory_space=pltpu.HBM)
    return pl.pallas_call(
        kernel,
        out_shape=pltpu.VMEM((ND, NC, SLOTS), f32),
        in_specs=[hbm] * 6,
        out_specs=pl.BlockSpec(memory_space=pltpu.VMEM),
        scratch_shapes=[
            pltpu.VMEM((1, ROWS, 1024), f32),
            pltpu.VMEM((1, ROWS, 1024), f32),
            pltpu.VMEM((ROWS, 1024), jnp.int32),
            pltpu.VMEM((48, 128), jnp.int32),
            pltpu.SMEM((NL,), jnp.int32),
            pltpu.SMEM((2, ND), f32),
            dma((7,)),
            pltpu.VMEM((ND, NC, SLOTS), f32),
            pltpu.VMEM((ND, NC, SLOTS), f32),
            pltpu.VMEM((NL, TILES) + vreg, f32),
            pltpu.VMEM((EARLY, NL) + vreg, f32),
            pltpu.VMEM((TILES, NL) + vreg, f32),
            pltpu.VMEM((TILES, 2, 128, 128), f32),
            pltpu.VMEM((EARLY, NL) + vreg, f32),
            pltpu.VMEM((TILES, NL) + vreg, f32),
            pltpu.VMEM((ND, NC, SLOTS), f32),
            pltpu.VMEM((2, ND, ROWS + 4) + vreg, f32),
            pltpu.VMEM((ND, ROWS) + vreg, f32),
            pltpu.VMEM((ND, ROWS) + vreg, f32),
            pltpu.VMEM((64, 128), f32),
            pltpu.VMEM((64, 128), f32),
            pltpu.VMEM((64, 128), f32),
            pltpu.VMEM((4,) + vreg, f32),
            pltpu.VMEM((ROWS,) + vreg, f32),
            pltpu.VMEM((ROWS + 1,) + vreg, f32),
            pltpu.VMEM((TILES,) + vreg, jnp.int32),
            pltpu.VMEM((TILES,) + vreg, jnp.int32),
            pltpu.VMEM((6,) + vreg, jnp.int32),
            pltpu.VMEM((6,) + vreg, jnp.int32),
            pltpu.VMEM((6,) + vreg, jnp.int32),
            pltpu.VMEM((6,) + vreg, jnp.int32),
            pltpu.VMEM((ROWS,) + vreg, jnp.int32),
            pltpu.VMEM((ROWS,) + vreg, jnp.int32),
            pltpu.VMEM((ROWS,) + vreg, jnp.int32),
            pltpu.VMEM((ROWS,) + vreg, jnp.int32),
            pltpu.VMEM((3, 2) + vreg, jnp.int32),
            pltpu.VMEM((3, 2) + vreg, jnp.int32),
            pltpu.VMEM((TILES,) + vreg, f32),
            dma((TILES,)), dma((TILES,)), dma((TILES,)),
            dma((TILES,)), dma((TILES,)), dma((TILES,)),
            dma((EARLY,)), dma((EARLY,)), dma((EARLY,)),
            dma((EARLY,)), dma((EARLY,)), dma((EARLY,)),
            dma((4,)), dma((4,)), dma((2, HALOS)), dma((2, HALOS)),
            dma((TILES,)), dma((TILES,)), dma((TILES,)),
            dma((TILES,)), dma((TILES,)), dma((TILES,)),
        ],
        compiler_params=pltpu.CompilerParams(
            collective_id=0, has_side_effects=True, vmem_limit_bytes=64000 * 1024
        ),
        name="wave_step",
    )(
        spectra_in.transpose(1, 0, 2),
        group_speed,
        turn_rate,
        sea_mask,
        sea_cell.reshape(48, 128),
        slab_counts,
    ).transpose(1, 0, 2)


def solution(mesh):
    in_specs = (
        P(None, None, ("comp", "lat")),
        P("comp", "lat", None),
        P("comp", "lat", None),
        P("lat", None),
        P("lat"),
        P(),
    )
    out_specs = P(None, None, ("comp", "lat"))
    return jax.shard_map(
        per_device, mesh=mesh, in_specs=in_specs, out_specs=out_specs, check_vma=False
    )
```
